512 devices in a mesh: dp: 8 (over z_hi, core), pipe: 8 (over z_lo, x), tensor: 8 (over y).
Axes of the slice: x: 4, y: 8, z: 8 (z_hi: 4, z_lo: 2; z = z_hi * 2 + z_lo), core: 2. Of those that a mesh axis runs over, the one named last changes fastest.
Arguments:
- normed: bfloat16 [8, 1024, 8192], P('pipe', 'tensor', 'dp'), may hold values from -6 to 6
- w_query: bfloat16 [8, 8192, 4096], P('pipe', 'dp', 'tensor'), may hold values from -0.0625 to 0.0625
- neighbour_kv: bfloat16 [8, 8, 8, 2, 128, 4096], P('dp', None, 'pipe', None, None, 'tensor'), may hold values from -190 to 190
- counts: int32 [8, 8, 2], P('pipe', 'dp'), may hold values from 1 to 4
- w_out: bfloat16 [8, 4096, 8192], P('pipe', 'tensor', 'dp'), may hold values from -0.75 to 0.75
Outputs:
- mixed: bfloat16 [8, 1024, 8192], P('pipe', 'tensor', 'dp')
The draws below stay inside these ranges and needn't reach their ends.
All inputs are finite; a program needn't handle non-finite values.
Results may differ from the reference program's by a relative error of at most 0.025.
Values may be sent and summed in bfloat16 or wider, within the bound.
A program may use at most 64 MiB of HBM per device.

```python
import math
import jax
import jax.numpy as jnp
from jax import lax

D = 8192
HEADS = 32
HD = 128
SPAN = 64
NLEN = 128
SLOTS = 4
CH_DEV = 2
TOK_S = 1024
N_DP = 8
N_PIPE = 8
N_TENSOR = 8


def draw_neighbour_kv(key, part):
    key = jax.random.fold_in(key, 11)
    full_shape = (N_PIPE, N_DP, CH_DEV * SLOTS, 2, NLEN, HEADS * HD)
    base_key = jax.random.fold_in(key, 0)
    values = jax.random.normal(base_key, full_shape, jnp.float32)
    values = jnp.clip(values, -6.0, 6.0)
    return values.astype(jnp.bfloat16)


def place_ends(array, rng, low, high):
    extent = array.shape
    place = [jax.random.randint(jax.random.fold_in(rng, axis), (), 0, extent[axis]) for axis in range(len(extent))]
    array = array.at[tuple(place)].set(low)
    longest = extent.index(max(extent))
    place[longest] = (place[longest] + 1) % extent[longest]
    return array.at[tuple(place)].set(high)


def level_of(key, shape, cuts, smallest, high):
    def one(dim, shards_of):
        heights = jax.random.uniform(jax.random.fold_in(jax.random.fold_in(key, 6), dim), (shards_of,), jnp.float32, smallest / len(cuts), high / len(cuts))
        return jnp.repeat(jnp.exp(heights), shape[dim] // shards_of).reshape((-1,) + (1,) * (len(shape) - dim - 1))

    level = one(*cuts[0])
    for cut in cuts[1:]:
        level = level * one(*cut)
    return level


def scatter_about(rng, dims, deviation, bound, cuts=(), held_as=jnp.bfloat16):
    drawn = deviation * jax.random.normal(rng, dims, jnp.float32)
    if cuts:
        drawn = drawn * level_of(rng, dims, cuts, -0.22, 0.18)
    return jnp.clip(drawn, -bound, bound).astype(held_as)


def setup_inputs(seed: int = 0) -> dict:
    key_list = jax.random.split(jax.random.key(seed), 6)
    normed = scatter_about(key_list[0], (N_PIPE, TOK_S, D), 1.0, 6.0, ((0, 8), (1, 8), (2, 8)))
    w_query = scatter_about(key_list[1], (N_PIPE, D, HEADS * HD), D ** -0.5, 0.0625, ((0, 8), (1, 8), (2, 8)))
    neighbour_kv = draw_neighbour_kv(jax.random.fold_in(key_list[5], 71), 0)
    counts = place_ends(jax.random.randint(key_list[3], (N_PIPE, N_DP, CH_DEV), 1, 5), jax.random.fold_in(key_list[3], 1), 1, 4).astype(jnp.int32)
    w_out = scatter_about(key_list[4], (N_PIPE, HEADS * HD, D), (HEADS * HD // 64) ** -0.5, 0.75, ((0, 8), (1, 8), (2, 8)))
    return dict(normed=normed, w_query=w_query, neighbour_kv=neighbour_kv, counts=counts, w_out=w_out)


def attend_blocks(queries, neighbours, head_count):
    block_count, row_count, feature_width = queries.shape
    head_size = feature_width // head_count
    key_length = neighbours.shape[2]
    query_heads = queries.astype(jnp.float32).reshape(block_count, row_count, head_count, head_size)
    key_heads = neighbours[:, 0].astype(jnp.float32).reshape(block_count, key_length, head_count, head_size)
    value_heads = neighbours[:, 1].astype(jnp.float32).reshape(block_count, key_length, head_count, head_size)
    scores = jnp.einsum('bihd,bjhd->bhij', query_heads, key_heads) * (1.0 / math.sqrt(head_size))
    block_max = lax.optimization_barrier(jnp.max(scores, axis=3))
    exponent = jnp.exp(scores - block_max[..., None])
    block_sum = lax.optimization_barrier(jnp.sum(exponent, axis=3))
    weights = exponent.astype(jnp.bfloat16).astype(jnp.float32)
    block_out = jnp.einsum('bhij,bjhd->bihd', weights, value_heads)
    return (block_max, block_sum, block_out.reshape(block_count, row_count, feature_width))

def combine_slots(block_max, block_sum, block_out, count_row, slot_count, head_count):
    span_count = count_row.shape[0]
    row_count = block_out.shape[1]
    feature_width = block_out.shape[2]
    head_size = feature_width // head_count
    slot_valid = jnp.arange(slot_count, dtype=jnp.int32)[None, :] < count_row[:, None]
    mask_full = slot_valid[:, :, None, None]
    block_max = block_max.reshape(span_count, slot_count, head_count, row_count)
    block_sum = block_sum.reshape(span_count, slot_count, head_count, row_count)
    span_max = lax.optimization_barrier(jnp.max(jnp.where(mask_full, block_max, -jnp.inf), axis=1))
    factor = jnp.where(mask_full, jnp.exp(block_max - span_max[:, None]), 0.0)
    denominator = lax.optimization_barrier(jnp.sum(factor * block_sum, axis=1))
    pieces = block_out.reshape(span_count, slot_count, row_count, head_count, head_size)
    factor_rows = jnp.transpose(factor, (0, 1, 3, 2))[..., None]
    numerator = lax.optimization_barrier(jnp.sum(factor_rows * pieces, axis=1))
    result = numerator / jnp.transpose(denominator, (0, 2, 1))[..., None]
    return result.reshape(span_count * row_count, feature_width).astype(jnp.bfloat16)

def reference(normed, w_query, neighbour_kv, counts, w_out):
    feature_width = HEADS * HD
    group_width = feature_width // N_TENSOR

    def one_section(section_at):
        queries = jnp.dot(normed[section_at], w_query[section_at], preferred_element_type=jnp.float32).astype(jnp.bfloat16)
        neighbours = neighbour_kv[section_at].reshape(N_DP * CH_DEV * SLOTS, 2, NLEN, feature_width)
        span_queries = queries.reshape(N_DP * CH_DEV, 1, SPAN, feature_width)
        block_queries = jnp.broadcast_to(span_queries, (N_DP * CH_DEV, SLOTS, SPAN, feature_width))
        block_queries = block_queries.reshape(N_DP * CH_DEV * SLOTS, SPAN, feature_width)
        block_max, block_sum, block_out = attend_blocks(block_queries, neighbours, HEADS)
        attended = combine_slots(block_max, block_sum, block_out, counts[section_at].reshape(N_DP * CH_DEV), SLOTS, HEADS)
        mixed = jnp.zeros((TOK_S, D), jnp.float32)
        for group_at in range(N_TENSOR):
            low = group_at * group_width
            partial_term = jnp.dot(attended[:, low:low + group_width], w_out[section_at, low:low + group_width], preferred_element_type=jnp.float32)
            rounded = lax.optimization_barrier(partial_term.astype(jnp.bfloat16))
            mixed = mixed + rounded.astype(jnp.float32)
        return mixed.astype(jnp.bfloat16)
    return lax.map(one_section, jnp.arange(N_PIPE, dtype=jnp.int32))
```

```python
import math

import jax
import jax.numpy as jnp
from jax import lax
from jax.experimental import pallas as pl
from jax.experimental.pallas import tpu as pltpu
from jax.sharding import PartitionSpec as P

MESH = pl.DeviceIdType.MESH
BF = jnp.bfloat16
F32 = jnp.float32
HD = 128
NEG = -3.0e38
NG = 8
NK = 4
ROWS = 16


def kernel(
    normed, wq_in, kv_in, counts, wo_in, out,
    xg, wq, kv, wo, qp, qin, qfull, po, st, pin, sin, att, ain, pm, rsb, rin, cnt,
    ld_sem, own_send, ag_send, ag_recv, qp_send, qin_recv, xa_send, xa_recv, po_send, st_send, pin_recv, sin_recv,
    at_send, ain_recv, rs_send, rs_recv, cnt_send, cnt_recv,
):
    d = lax.axis_index("dp")
    p = lax.axis_index("pipe")
    t = lax.axis_index("tensor")
    c = p // NK
    k = p % NK
    up = (t + 1) % NG
    dn = (t + NG - 1) % NG
    on_diag = d == p

    def local(src, dst, sem):
        return pltpu.make_async_copy(src, dst, sem)

    def remote(src, dst, ssem, rsem, dev):
        return pltpu.make_async_remote_copy(
            src_ref=src, dst_ref=dst, send_sem=ssem, recv_sem=rsem, device_id=dev, device_id_type=MESH
        )

    def reach(src, dst, ssem, rsem, dev, is_self):
        @pl.when(is_self)
        def _():
            local(src, dst, rsem).start()

        @pl.when(jnp.logical_not(is_self))
        def _():
            remote(src, dst, ssem, rsem, dev).start()

    def await_bytes(ref, sem):
        local(ref, ref, sem).wait()

    loads = [
        local(normed.at[0], xg.at[0, 0], ld_sem.at[0]),
        local(normed.at[1], xg.at[0, 1], ld_sem.at[1]),
        local(wq_in, wq, ld_sem.at[2]),
        local(kv_in, kv, ld_sem.at[3]),
        local(wo_in, wo, ld_sem.at[4]),
    ]
    for load in loads:
        load.start()

    barrier = pltpu.get_barrier_semaphore()

    def greet(dev):
        pl.semaphore_signal(barrier, inc=1, device_id=dev, device_id_type=MESH)

    greet((d, p, up))
    greet((d, p, dn))

    def greet_slots(j, carry):
        greet((d, c * NK + (k + j) % NK, t))
        return carry

    lax.fori_loop(1, NK, greet_slots, 0)

    def greet_plane(j, carry):
        @pl.when(jnp.logical_not(on_diag & (j == p)))
        def _():
            greet((p, j, t))

        @pl.when(jnp.logical_not(on_diag & (j == d)))
        def _():
            greet((j, d, t))

        return carry

    lax.fori_loop(0, NG, greet_plane, 0)

    @pl.when(on_diag)
    def _():
        pl.semaphore_wait(barrier, 2 + 3 + 14)

    @pl.when(jnp.logical_not(on_diag))
    def _():
        pl.semaphore_wait(barrier, 2 + 3 + 16)

    for half in range(2):
        loads[half].wait()
        remote(xg.at[0, half], xg.at[1, half], own_send.at[0, half], ag_recv.at[1, half], (d, p, up)).start()
        remote(xg.at[0, half], xg.at[2, half], own_send.at[1, half], ag_recv.at[2, half], (d, p, dn)).start()

    def send_counts(j, carry):
        b = (j + d) % NG
        reach(counts.at[b // NK], cnt.at[d], cnt_send.at[0], cnt_recv.at[0], (p, b, t), on_diag & (b == p))
        return carry

    lax.fori_loop(0, NG, send_counts, 0)
    loads[2].wait()

    def project(i):
        @pl.when(i >= 1)
        def _():
            upward = i % 2 == 1
            target = (d, p, jnp.where(upward, up, dn))
            later = jnp.minimum(i + 2, NG - 1)
            for half in range(2):
                await_bytes(xg.at[i, half], ag_recv.at[i, half])
                goes = (i <= 5) if half == 0 else ((i <= 4) | (i == 6))

                @pl.when(goes)
                def _():
                    remote(
                        xg.at[i, half], xg.at[later, half], ag_send.at[i, half], ag_recv.at[later, half], target
                    ).start()

        rows = xg[i].reshape(128, 1024)
        part = jnp.dot(rows, wq[...], preferred_element_type=F32).astype(BF)
        qp[i] = part.reshape(NG, ROWS, 512)

        def send(j, carry):
            b = (j + d) % NG
            reach(qp.at[i, b], qin.at[i, d], qp_send.at[i], qin_recv.at[i], (p, b, t), on_diag & (b == p))
            return carry

        lax.fori_loop(0, NG, send, 0)

    def total_query(i):
        await_bytes(qin.at[i], qin_recv.at[i])
        total = qin[i, 0].astype(F32)
        for n in range(1, NG):
            total = total + qin[i, n].astype(F32)
        qfull[i, k] = total.astype(BF)

        def send(j, carry):
            other = c * NK + (k + j) % NK
            remote(qfull.at[i, k], qfull.at[i, k], xa_send.at[i], xa_recv.at[i], (d, other, t)).start()
            return carry

        lax.fori_loop(1, NK, send, 0)

    def sequence_of(i):
        hop = (i + 1) // 2
        return (t + NG + jnp.where(i % 2 == 1, -hop, hop)) % NG

    def attend(i):
        @pl.when(i == 0)
        def _():
            loads[3].wait()
            await_bytes(cnt, cnt_recv.at[0])

        await_bytes(qfull.at[i, pl.ds(0, 3)], xa_recv.at[i])
        g = sequence_of(i)
        lane = lax.broadcasted_iota(jnp.int32, (64, 128), 1)

        def head(h, stats):
            cut = pl.ds(pl.multiple_of(h * HD, HD), HD)
            scores = lax.dot_general(
                qfull[i, :, :, cut].reshape(64, HD), kv[g, 0, :, cut], (((1,), (1,)), ((), ())),
                preferred_element_type=F32,
            ) * (1.0 / math.sqrt(HD))
            top = jnp.max(scores, axis=1, keepdims=True)
            e = jnp.exp(scores - top)
            total = jnp.sum(e, axis=1, keepdims=True)
            o = jnp.dot(e.astype(BF), kv[g, 1, :, cut], preferred_element_type=F32)
            po[i, :, :, cut] = o.astype(BF).reshape(NK, ROWS, HD)
            return jnp.where(lane == h, top, jnp.where(lane == 4 + h, total, stats))

        stats = lax.fori_loop(0, 4, head, jnp.zeros((64, 128), F32))
        stats = jnp.where((lane < 4) & (cnt[g][0:1, :] <= k), NEG, stats)
        st[i] = stats.reshape(NK, ROWS, 128)
        pin[i, k] = po[i, k]
        sin[i, k] = st[i, k]

        def send(j, carry):
            k2 = (k + j) % NK
            dev = (d, c * NK + k2, t)
            remote(po.at[i, k2], pin.at[i, k], po_send.at[i], pin_recv.at[i], dev).start()
            remote(st.at[i, k2], sin.at[i, k], st_send.at[i], sin_recv.at[i], dev).start()
            return carry

        lax.fori_loop(1, NK, send, 0)

    def combine(i):
        await_bytes(pin.at[i, pl.ds(0, 3)], pin_recv.at[i])
        await_bytes(sin.at[i, pl.ds(0, 3)], sin_recv.at[i])
        stats = [sin[i, n] for n in range(NK)]
        top = jnp.maximum(jnp.maximum(stats[0], stats[1]), jnp.maximum(stats[2], stats[3]))
        factor = [jnp.exp(s - top) for s in stats]
        den = factor[0] * pltpu.roll(stats[0], 124, 1)
        for n in range(1, NK):
            den = den + factor[n] * pltpu.roll(stats[n], 124, 1)
        weight = [f / den for f in factor]
        for h in range(4):
            cut = slice(h * HD, (h + 1) * HD)
            num = weight[0][:, h:h + 1] * pin[i, 0, :, cut].astype(F32)
            for n in range(1, NK):
                num = num + weight[n][:, h:h + 1] * pin[i, n, :, cut].astype(F32)
            att[i, :, cut] = num.astype(BF)

        def send(j, carry):
            d2 = (j + p) % NG
            reach(att.at[i], ain.at[i, p], at_send.at[i], ain_recv.at[i], (d2, d, t), on_diag & (d2 == d))
            return carry

        lax.fori_loop(0, NG, send, 0)

    def mix(i):
        @pl.when(i == 0)
        def _():
            loads[4].wait()

        await_bytes(ain.at[i], ain_recv.at[i])
        pm[i] = jnp.dot(ain[i].reshape(128, 512), wo[...], preferred_element_type=F32)

    def step(i, carry):
        for lag, stage in enumerate((project, total_query, attend, combine, mix)):
            @pl.when((i >= lag) & (i - lag < NG))
            def _():
                stage(i - lag)

        return carry

    lax.fori_loop(0, NG + 4, step, 0)

    def pass_on(slot, half, later, tensor_to, incoming):
        mine = pm[slot, :, half * 512:(half + 1) * 512]
        if incoming:
            await_bytes(rin.at[slot, half], rs_recv.at[slot, half])
            mine = mine + rin[slot, half].astype(F32)
        rsb[slot, half] = mine.astype(BF)
        remote(
            rsb.at[slot, half], rin.at[later, half], rs_send.at[slot, half], rs_recv.at[later, half],
            (d, p, tensor_to),
        ).start()

    pass_on(7, 0, 5, dn, False)
    pass_on(7, 1, 6, up, False)
    pass_on(5, 1, 3, dn, False)
    pass_on(6, 0, 4, up, False)
    pass_on(5, 0, 3, dn, True)
    pass_on(6, 1, 4, up, True)
    for half in range(2):
        pass_on(3, 1 - half, 1, dn, True)
        pass_on(4, half, 2, up, True)
    for half in range(2):
        pass_on(1, 1 - half, 0, dn, True)
        pass_on(2, half, 7, up, True)
    for half in range(2):
        await_bytes(rin.at[0, half], rs_recv.at[0, half])
        await_bytes(rin.at[7, half], rs_recv.at[7, half])
        cut = slice(half * 512, (half + 1) * 512)
        out[:, cut] = (pm[0, :, cut] + rin[0, half].astype(F32) + rin[7, half].astype(F32)).astype(BF)

    for way in range(2):
        for half in range(2):
            await_bytes(xg.at[0, half], own_send.at[way, half])
    for i in range(1, 7):
        for half in range(2):
            if (half == 0 and i <= 5) or (half == 1 and i != 5):
                await_bytes(xg.at[i, half], ag_send.at[i, half])
    for slot in range(1, NG):
        for half in range(2):
            await_bytes(rsb.at[slot, half], rs_send.at[slot, half])

    @pl.when(on_diag)
    def _():
        await_bytes(cnt.at[pl.ds(0, 7)], cnt_send.at[0])

    @pl.when(jnp.logical_not(on_diag))
    def _():
        await_bytes(cnt, cnt_send.at[0])

    def drain(i, carry):
        await_bytes(qfull.at[i, pl.ds(0, 3)], xa_send.at[i])
        await_bytes(po.at[i, pl.ds(0, 3)], po_send.at[i])
        await_bytes(st.at[i, pl.ds(0, 3)], st_send.at[i])

        @pl.when(on_diag)
        def _():
            await_bytes(qp.at[i, pl.ds(0, 7)], qp_send.at[i])
            await_bytes(ain.at[i, pl.ds(0, 7)], at_send.at[i])

        @pl.when(jnp.logical_not(on_diag))
        def _():
            await_bytes(qp.at[i], qp_send.at[i])
            await_bytes(ain.at[i], at_send.at[i])

        return carry

    lax.fori_loop(0, NG, drain, 0)


def on_device(normed, w_query, neighbour_kv, counts, w_out):
    dma = pltpu.SemaphoreType.DMA
    anywhere = pl.BlockSpec(memory_space=pl.ANY)
    return pl.pallas_call(
        kernel,
        out_shape=jax.ShapeDtypeStruct((128, 1024), BF),
        in_specs=[anywhere, anywhere, anywhere, pl.BlockSpec(memory_space=pltpu.VMEM), anywhere],
        out_specs=pl.BlockSpec(memory_space=pltpu.VMEM),
        scratch_shapes=[
            pltpu.VMEM((NG, 2, 64, 1024), BF),
            pltpu.VMEM((1024, 512), BF),
            pltpu.VMEM((NG, 2, 128, 512), BF),
            pltpu.VMEM((512, 1024), BF),
            pltpu.VMEM((NG, NG, ROWS, 512), BF),
            pltpu.VMEM((NG, NG, ROWS, 512), BF),
            pltpu.VMEM((NG, NK, ROWS, 512), BF),
            pltpu.VMEM((NG, NK, ROWS, 512), BF),
            pltpu.VMEM((NG, NK, ROWS, 128), F32),
            pltpu.VMEM((NG, NK, ROWS, 512), BF),
            pltpu.VMEM((NG, NK, ROWS, 128), F32),
            pltpu.VMEM((NG, ROWS, 512), BF),
            pltpu.VMEM((NG, NG, ROWS, 512), BF),
            pltpu.VMEM((NG, 128, 1024), F32),
            pltpu.VMEM((NG, 2, 128, 512), BF),
            pltpu.VMEM((NG, 2, 128, 512), BF),
            pltpu.VMEM((NG, 8, 128), jnp.int32),
            dma((5,)), dma((2, 2)), dma((NG, 2)), dma((NG, 2)),
            dma((NG,)), dma((NG,)), dma((NG,)), dma((NG,)),
            dma((NG,)), dma((NG,)), dma((NG,)), dma((NG,)),
            dma((NG,)), dma((NG,)), dma((NG, 2)), dma((NG, 2)),
            dma((1,)), dma((1,)),
        ],
        compiler_params=pltpu.CompilerParams(
            collective_id=0, has_side_effects=True, vmem_limit_bytes=60 * 1024 * 1024
        ),
        cost_estimate=pl.CostEstimate(flops=2_500_000_000, bytes_accessed=5_000_000, transcendentals=300_000),
    )(
        normed.reshape(2, 64, 1024),
        w_query.reshape(1024, 512),
        neighbour_kv.reshape(NG, 2, 128, 512),
        jnp.broadcast_to(counts.reshape(2, 1, 1), (2, 8, 128)),
        w_out.reshape(512, 1024),
    )[None]


def solution(mesh):
    return jax.shard_map(
        on_device,
        mesh=mesh,
        in_specs=(
            P("pipe", "tensor", "dp"),
            P("pipe", "dp", "tensor"),
            P("dp", None, "pipe", None, None, "tensor"),
            P("pipe", "dp", None),
            P("pipe", "tensor", "dp"),
        ),
        out_specs=P("pipe", "tensor", "dp"),
        check_vma=False,
    )
```

```python
import math

import jax
import jax.numpy as jnp
from jax import lax
from jax.experimental import pallas as pl
from jax.experimental.pallas import tpu as pltpu
from jax.sharding import PartitionSpec as P

MESH = pl.DeviceIdType.MESH
BF = jnp.bfloat16
F32 = jnp.float32
HD = 128
NEG = -3.0e38
NG = 8
NK = 4
ROWS = 16
UNITS = 2 * NG
LAGS = (0, 2, 4, 6, 8, 10, 12, 14)
BY_SPAN = False
RING_AT = {}


def kernel(
    normed, wq_in, kv_in, counts, wo_in, out,
    xg, wq, kv, wo, qp, sib, qs, qin, qfull, po, st, pin, sin, att, ain, pm, rsb, rin, cnt_two, cnt,
    ld_sem, own_send, ag_send, ag_recv, sib_send, sib_recv, qs_send, qin_recv, xa_send, xa_recv,
    po_send, st_send, pin_recv, sin_recv, at_send, at_recv, sp_send, sp_recv, fw_send, fw_recv,
    rs_send, rs_recv, c2_send, c2_recv, cnt_send, cnt_recv,
):
    d = lax.axis_index("dp")
    p = lax.axis_index("pipe")
    t = lax.axis_index("tensor")
    zh = d // 2
    co = d % 2
    sibling = d + 1 - 2 * co
    c_own = p // NK
    k = p % NK
    up = (t + 1) % NG
    dn = (t + NG - 1) % NG
    on_diag = d == p
    query_self = on_diag & (k // 2 == co)
    spread_self = on_diag & (2 * k + c_own == d)

    def local(src, dst, sem):
        return pltpu.make_async_copy(src, dst, sem)

    def remote(src, dst, ssem, rsem, dev):
        return pltpu.make_async_remote_copy(
            src_ref=src, dst_ref=dst, send_sem=ssem, recv_sem=rsem, device_id=dev, device_id_type=MESH
        )

    def reach(src, dst, ssem, rsem, dev, is_self):
        @pl.when(is_self)
        def _():
            local(src, dst, rsem).start()

        @pl.when(jnp.logical_not(is_self))
        def _():
            remote(src, dst, ssem, rsem, dev).start()

    def await_bytes(ref, sem):
        local(ref, ref, sem).wait()

    loads = [
        local(normed.at[0], xg.at[0, 0], ld_sem.at[0]),
        local(normed.at[1], xg.at[0, 1], ld_sem.at[1]),
        local(wq_in, wq, ld_sem.at[2]),
        local(kv_in, kv, ld_sem.at[3]),
        local(wo_in, wo, ld_sem.at[4]),
    ]
    for load in loads:
        load.start()

    barrier = pltpu.get_barrier_semaphore()

    def greet(dev):
        pl.semaphore_signal(barrier, inc=1, device_id=dev, device_id_type=MESH)

    def greet_other(dev, is_self):
        @pl.when(jnp.logical_not(is_self))
        def _():
            greet(dev)

    greet((d, p, up))
    greet((d, p, dn))
    for n in range(NK):
        b = (n % 2) * NK + 2 * co + n // 2
        greet_other((p, b, t), on_diag & (b == p))
        source = 2 * n + k // 2
        greet_other((source, d, t), on_diag & (source == d))
    greet_other((2 * k + c_own, d, t), spread_self)
    greet_other((p, NK * co + zh, t), spread_self)
    for n in range(1, NK):
        greet((d, c_own * NK + (k + n) % NK, t))
        greet((((zh + n) % NK) * 2 + co, p, t))
    greet((sibling, p, t))
    for span in range(2):
        cnt_two[span, co] = jnp.full((8, 128), counts[0, 0, span], jnp.int32)
    pl.semaphore_wait(barrier, 19 - 2 * jnp.where(query_self, 1, 0) - 2 * jnp.where(spread_self, 1, 0))

    for half in range(2):
        loads[half].wait()
        remote(xg.at[0, half], xg.at[1, half], own_send.at[0, half], ag_recv.at[1, half], (d, p, up)).start()
        remote(xg.at[0, half], xg.at[2, half], own_send.at[1, half], ag_recv.at[2, half], (d, p, dn)).start()
    for span in range(2):
        remote(
            cnt_two.at[span, co], cnt_two.at[span, co], c2_send.at[span], c2_recv.at[span], (sibling, p, t)
        ).start()
    loads[2].wait()

    def project(c, i):
        @pl.when(i >= 1)
        def _():
            await_bytes(xg.at[i, c], ag_recv.at[i, c])
            upward = i % 2 == 1
            target = (d, p, jnp.where(upward, up, dn))
            later = jnp.minimum(i + 2, NG - 1)

            @pl.when((i <= 4) | (i == 5 + c))
            def _():
                remote(xg.at[i, c], xg.at[later, c], ag_send.at[i, c], ag_recv.at[later, c], target).start()

        part = jnp.dot(xg[i, c], wq[...], preferred_element_type=F32).astype(BF)
        qp[c, i] = part.reshape(NK, ROWS, 512)
        remote(
            qp.at[c, i, pl.ds(2 - 2 * co, 2)], sib.at[c, i], sib_send.at[c, i], sib_recv.at[c, i], (sibling, p, t)
        ).start()

    def join_cores(c, i):
        @pl.when(i == 0)
        def _():
            await_bytes(cnt_two.at[c, co], c2_recv.at[c])
            for n in range(2):
                b = c * NK + 2 * co + n
                reach(cnt_two.at[c], cnt.at[zh], cnt_send.at[c], cnt_recv.at[0], (p, b, t), on_diag & (b == p))

        await_bytes(sib.at[c, i], sib_recv.at[c, i])
        for n in range(2):
            b = c * NK + 2 * co + n
            qs[c, i, n] = (qp[c, i, 2 * co + n].astype(F32) + sib[c, i, n].astype(F32)).astype(BF)
            reach(qs.at[c, i, n], qin.at[i, zh], qs_send.at[c, i], qin_recv.at[i], (p, b, t), on_diag & (b == p))

    def total_query(c, i):
        await_bytes(qin.at[i], qin_recv.at[i])
        total = qin[i, 0].astype(F32)
        for n in range(1, NK):
            total = total + qin[i, n].astype(F32)
        qfull[i, k] = total.astype(BF)
        for n in range(1, NK):
            dev = (d, c_own * NK + (k + n) % NK, t)
            remote(qfull.at[i, k], qfull.at[i, k], xa_send.at[i], xa_recv.at[i], dev).start()

    def sequence_of(i):
        hop = (i + 1) // 2
        return (t + NG + jnp.where(i % 2 == 1, -hop, hop)) % NG

    def attend(c, i):
        @pl.when(i == 0)
        def _():
            loads[3].wait()
            await_bytes(cnt, cnt_recv.at[0])

        await_bytes(qfull.at[i, pl.ds(0, 3)], xa_recv.at[i])
        g = sequence_of(i)
        lane = lax.broadcasted_iota(jnp.int32, (64, 128), 1)
        stats = jnp.zeros((64, 128), F32)
        for h in range(4):
            cut = slice(h * HD, (h + 1) * HD)
            scores = lax.dot_general(
                qfull[i, :, :, cut].reshape(64, HD), kv[g, 0, :, cut], (((1,), (1,)), ((), ())),
                preferred_element_type=F32,
            ) * (1.0 / math.sqrt(HD))
            top = jnp.max(scores, axis=1, keepdims=True)
            e = jnp.exp(scores - top)
            total = jnp.sum(e, axis=1, keepdims=True)
            o = jnp.dot(e.astype(BF), kv[g, 1, :, cut], preferred_element_type=F32)
            po[i, :, :, cut] = o.astype(BF).reshape(NK, ROWS, HD)
            stats = jnp.where(lane == h, top, stats)
            stats = jnp.where(lane == 4 + h, total, stats)
        stats = jnp.where((lane < 4) & (cnt[g // 2, g % 2][0:1, :] <= k), NEG, stats)
        st[i] = stats.reshape(NK, ROWS, 128)
        pin[i, k] = po[i, k]
        sin[i, k] = st[i, k]
        for n in range(1, NK):
            k2 = (k + n) % NK
            dev = (d, c_own * NK + k2, t)
            remote(po.at[i, k2], pin.at[i, k], po_send.at[i], pin_recv.at[i], dev).start()
            remote(st.at[i, k2], sin.at[i, k], st_send.at[i], sin_recv.at[i], dev).start()

    def combine(c, i):
        await_bytes(pin.at[i, pl.ds(0, 3)], pin_recv.at[i])
        await_bytes(sin.at[i, pl.ds(0, 3)], sin_recv.at[i])
        stats = [sin[i, n] for n in range(NK)]
        top = jnp.maximum(jnp.maximum(stats[0], stats[1]), jnp.maximum(stats[2], stats[3]))
        factor = [jnp.exp(s - top) for s in stats]
        den = factor[0] * pltpu.roll(stats[0], 124, 1)
        for n in range(1, NK):
            den = den + factor[n] * pltpu.roll(stats[n], 124, 1)
        weight = [f / den for f in factor]
        for h in range(4):
            cut = slice(h * HD, (h + 1) * HD)
            num = weight[0][:, h:h + 1] * pin[i, 0, :, cut].astype(F32)
            for n in range(1, NK):
                num = num + weight[n][:, h:h + 1] * pin[i, n, :, cut].astype(F32)
            att[i, :, cut] = num.astype(BF)
        reach(att.at[i], ain.at[c_own, i, k], at_send.at[i], at_recv.at[i], (2 * k + c_own, d, t), spread_self)

    def spread(c, i):
        await_bytes(att.at[i], at_recv.at[i])
        for n in range(1, NK):
            dev = (((zh + n) % NK) * 2 + co, p, t)
            remote(ain.at[co, i, zh], ain.at[co, i, zh], sp_send.at[i], sp_recv.at[i], dev).start()

    def hand_over(c, i):
        await_bytes(ain.at[co, i, pl.ds(0, 3)], sp_recv.at[i])
        remote(ain.at[co, i], ain.at[co, i], fw_send.at[i], fw_recv.at[i], (sibling, p, t)).start()

    def mix(c, i):
        @pl.when((c == 0) & (i == 0))
        def _():
            loads[4].wait()

        @pl.when(co != c)
        def _():
            await_bytes(ain.at[c, i], fw_recv.at[i])

        pm[c, i] = jnp.dot(ain[c, i].reshape(64, 512), wo[...], preferred_element_type=F32)

    def pass_on(c, slot, later, tensor_to, incoming):
        mine = pm[c, slot]
        if incoming:
            await_bytes(rin.at[c, slot], rs_recv.at[c, slot])
            mine = mine + rin[c, slot].astype(F32)
        rsb[c, slot] = mine.astype(BF)
        remote(
            rsb.at[c, slot], rin.at[c, later], rs_send.at[c, slot], rs_recv.at[c, later], (d, p, tensor_to)
        ).start()

    def ring(c, r):
        down = {1: (5, 3), 2: (3, 1), 3: (1, 0)}
        upward = {1: (6, 4), 2: (4, 2), 3: (2, 7)}
        if r == 0 and c == 0:
            pass_on(c, 7, 5, dn, False)
            pass_on(c, 6, 4, up, False)
        elif r == 0:
            pass_on(c, 7, 6, up, False)
            pass_on(c, 5, 3, dn, False)
        elif r == 1 and c == 0:
            pass_on(c, *down[r], dn, True)
        elif r == 1:
            pass_on(c, *upward[r], up, True)
        elif r < 4:
            pass_on(c, *down[r], dn, True)
            pass_on(c, *upward[r], up, True)
        else:
            await_bytes(rin.at[c, 0], rs_recv.at[c, 0])
            await_bytes(rin.at[c, 7], rs_recv.at[c, 7])
            out[c * 64:(c + 1) * 64] = (pm[c, 0] + rin[c, 0].astype(F32) + rin[c, 7].astype(F32)).astype(BF)

    stages = (
        (project, None), (join_cores, None), (total_query, c_own), (attend, c_own), (combine, c_own),
        (spread, co), (hand_over, co), (mix, None),
    )

    def step(u, carry):
        for lag, (stage, only) in zip(LAGS, stages):
            v = u - lag
            c, i = (v // NG, v % NG) if BY_SPAN else (v % 2, v // 2)
            run = (v >= 0) & (v < UNITS)

            @pl.when(run if only is None else run & (c == only))
            def _():
                stage(c, i)

        for (c, r), at in RING_AT.items():
            @pl.when(u == at)
            def _():
                ring(c, r)

        return carry

    lax.fori_loop(0, UNITS + LAGS[-1], step, 0)
    for r in range(5):
        for c in range(2):
            if (c, r) not in RING_AT:
                ring(c, r)

    for way in range(2):
        for half in range(2):
            await_bytes(xg.at[0, half], own_send.at[way, half])
    for i in range(1, 7):
        for half in range(2):
            if i <= 4 or i == 5 + half:
                await_bytes(xg.at[i, half], ag_send.at[i, half])
    for c in range(2):
        await_bytes(cnt_two.at[c, co], c2_send.at[c])

    def drain(i, carry):
        for c in range(2):
            @pl.when(i >= 1)
            def _():
                await_bytes(rsb.at[c, i], rs_send.at[c, i])

            await_bytes(sib.at[c, i], sib_send.at[c, i])
            one_less = query_self & (c == c_own)

            @pl.when(one_less)
            def _():
                await_bytes(qs.at[c, i, 0], qs_send.at[c, i])

            @pl.when(jnp.logical_not(one_less))
            def _():
                await_bytes(qs.at[c, i], qs_send.at[c, i])

            @pl.when((i == 0) & one_less)
            def _():
                await_bytes(cnt.at[0], cnt_send.at[c])

            @pl.when((i == 0) & jnp.logical_not(one_less))
            def _():
                await_bytes(cnt.at[pl.ds(0, 2)], cnt_send.at[c])

        await_bytes(qfull.at[i, pl.ds(0, 3)], xa_send.at[i])
        await_bytes(po.at[i, pl.ds(0, 3)], po_send.at[i])
        await_bytes(st.at[i, pl.ds(0, 3)], st_send.at[i])

        @pl.when(jnp.logical_not(spread_self))
        def _():
            await_bytes(att.at[i], at_send.at[i])

        await_bytes(ain.at[0, i, pl.ds(0, 3)], sp_send.at[i])
        await_bytes(ain.at[0, i], fw_send.at[i])
        return carry

    lax.fori_loop(0, NG, drain, 0)


def on_device(normed, w_query, neighbour_kv, counts, w_out):
    dma = pltpu.SemaphoreType.DMA
    anywhere = pl.BlockSpec(memory_space=pl.ANY)
    both = dma((2, NG))
    one = dma((NG,))
    return pl.pallas_call(
        kernel,
        out_shape=jax.ShapeDtypeStruct((128, 1024), BF),
        in_specs=[anywhere, anywhere, anywhere, pl.BlockSpec(memory_space=pltpu.SMEM), anywhere],
        out_specs=pl.BlockSpec(memory_space=pltpu.VMEM),
        scratch_shapes=[
            pltpu.VMEM((NG, 2, 64, 1024), BF),
            pltpu.VMEM((1024, 512), BF),
            pltpu.VMEM((NG, 2, 128, 512), BF),
            pltpu.VMEM((512, 1024), BF),
            pltpu.VMEM((2, NG, NK, ROWS, 512), BF),
            pltpu.VMEM((2, NG, 2, ROWS, 512), BF),
            pltpu.VMEM((2, NG, 2, ROWS, 512), BF),
            pltpu.VMEM((NG, NK, ROWS, 512), BF),
            pltpu.VMEM((NG, NK, ROWS, 512), BF),
            pltpu.VMEM((NG, NK, ROWS, 512), BF),
            pltpu.VMEM((NG, NK, ROWS, 128), F32),
            pltpu.VMEM((NG, NK, ROWS, 512), BF),
            pltpu.VMEM((NG, NK, ROWS, 128), F32),
            pltpu.VMEM((NG, ROWS, 512), BF),
            pltpu.VMEM((2, NG, NK, ROWS, 512), BF),
            pltpu.VMEM((2, NG, 64, 1024), F32),
            pltpu.VMEM((2, NG, 64, 1024), BF),
            pltpu.VMEM((2, NG, 64, 1024), BF),
            pltpu.VMEM((2, 2, 8, 128), jnp.int32),
            pltpu.VMEM((NK, 2, 8, 128), jnp.int32),
            dma((5,)), dma((2, 2)), dma((NG, 2)), dma((NG, 2)),
            both, both, both, one, one, one,
            one, one, one, one, one, one, one, one, one, one,
            both, both, dma((2,)), dma((2,)), dma((2,)), dma((1,)),
        ],
        compiler_params=pltpu.CompilerParams(
            collective_id=0, has_side_effects=True, vmem_limit_bytes=60 * 1024 * 1024
        ),
        cost_estimate=pl.CostEstimate(flops=2_500_000_000, bytes_accessed=5_000_000, transcendentals=300_000),
    )(
        normed.reshape(2, 64, 1024),
        w_query.reshape(1024, 512),
        neighbour_kv.reshape(NG, 2, 128, 512),
        counts,
        w_out.reshape(512, 1024),
    )[None]


def solution(mesh):
    return jax.shard_map(
        on_device,
        mesh=mesh,
        in_specs=(
            P("pipe", "tensor", "dp"),
            P("pipe", "dp", "tensor"),
            P("dp", None, "pipe", None, None, "tensor"),
            P("pipe", "dp", None),
            P("pipe", "tensor", "dp"),
        ),
        out_specs=P("pipe", "tensor", "dp"),
        check_vma=False,
    )
```

```python
import math

import jax
import jax.numpy as jnp
from jax import lax
from jax.experimental import pallas as pl
from jax.experimental.pallas import tpu as pltpu
from jax.sharding import PartitionSpec as P

MESH = pl.DeviceIdType.MESH
BF = jnp.bfloat16
F32 = jnp.float32
HD = 128
NEG = -3.0e38
NG = 8
NK = 4
UNITS = 2 * NG
LAGS = (0, 2, 5, 8, 10)
BY_SPAN = False
RING_AT = {}


def kernel(
    normed, wq_in, kv_in, counts, wo_in, out,
    xg, wq, kv, kvh, wo, qp, sib, qs, qin, att, ain, pm, rsb, rin, cnt_two, cnt,
    ld_sem, own_send, ag_send, ag_recv, sib_send, sib_recv, qs_send, qin_recv, kv_own, kv_send, kv_recv,
    at_send, at_recv, fw_send, fw_recv, rs_send, rs_recv, c2_send, c2_recv, cnt_send, cnt_recv,
):
    d = lax.axis_index("dp")
    p = lax.axis_index("pipe")
    t = lax.axis_index("tensor")
    zh = d // 2
    co = d % 2
    sibling = d + 1 - 2 * co
    c_own = p // NK
    k = p % NK
    up = (t + 1) % NG
    dn = (t + NG - 1) % NG
    on_diag = d == p
    query_self = on_diag & (k // 2 == co)

    def local(src, dst, sem):
        return pltpu.make_async_copy(src, dst, sem)

    def remote(src, dst, ssem, rsem, dev):
        return pltpu.make_async_remote_copy(
            src_ref=src, dst_ref=dst, send_sem=ssem, recv_sem=rsem, device_id=dev, device_id_type=MESH
        )

    def reach(src, dst, ssem, rsem, dev, is_self):
        @pl.when(is_self)
        def _():
            local(src, dst, rsem).start()

        @pl.when(jnp.logical_not(is_self))
        def _():
            remote(src, dst, ssem, rsem, dev).start()

    def await_bytes(ref, sem):
        local(ref, ref, sem).wait()

    loads = [
        local(normed.at[0], xg.at[0, 0], ld_sem.at[0]),
        local(normed.at[1], xg.at[0, 1], ld_sem.at[1]),
        local(wq_in, wq, ld_sem.at[2]),
        local(kv_in, kv, ld_sem.at[3]),
        local(wo_in, wo, ld_sem.at[4]),
    ]
    for load in loads:
        load.start()

    barrier = pltpu.get_barrier_semaphore()

    def greet(dev):
        pl.semaphore_signal(barrier, inc=1, device_id=dev, device_id_type=MESH)

    def greet_other(dev, is_self):
        @pl.when(jnp.logical_not(is_self))
        def _():
            greet(dev)

    greet((d, p, up))
    greet((d, p, dn))
    for n in range(NK):
        b = (n % 2) * NK + 2 * co + n // 2
        greet_other((p, b, t), on_diag & (b == p))
        source = 2 * n + k // 2
        greet_other((source, d, t), on_diag & (source == d))
    for n in range(1, NK):
        greet((d, c_own * NK + (k + n) % NK, t))
    greet((sibling, p, t))
    for span in range(2):
        cnt_two[span, co] = jnp.full((8, 128), counts[0, 0, span], jnp.int32)
    pl.semaphore_wait(barrier, 14 - 2 * jnp.where(query_self, 1, 0))

    for half in range(2):
        loads[half].wait()
        remote(xg.at[0, half], xg.at[1, half], own_send.at[0, half], ag_recv.at[1, half], (d, p, up)).start()
        remote(xg.at[0, half], xg.at[2, half], own_send.at[1, half], ag_recv.at[2, half], (d, p, dn)).start()
    for span in range(2):
        remote(
            cnt_two.at[span, co], cnt_two.at[span, co], c2_send.at[span], c2_recv.at[span], (sibling, p, t)
        ).start()
    loads[3].wait()

    def sequence_of(i):
        hop = (i + 1) // 2
        return (t + NG + jnp.where(i % 2 == 1, -hop, hop)) % NG

    def head_of(n):
        return pl.ds(pl.multiple_of(n * HD, HD), HD)

    def send_heads(i, carry):
        g = sequence_of(i)
        local(kv.at[g, :, :, head_of(k)], kvh.at[i, :, k], kv_own.at[i]).start()
        for n in range(1, NK):
            k2 = (k + n) % NK
            remote(
                kv.at[g, :, :, head_of(k2)], kvh.at[i, :, k], kv_send.at[i], kv_recv.at[i],
                (d, c_own * NK + k2, t),
            ).start()
        return carry

    lax.fori_loop(0, NG, send_heads, 0)
    loads[2].wait()

    def project(c, i):
        @pl.when(i >= 1)
        def _():
            await_bytes(xg.at[i, c], ag_recv.at[i, c])
            upward = i % 2 == 1
            target = (d, p, jnp.where(upward, up, dn))
            later = jnp.minimum(i + 2, NG - 1)

            @pl.when((i <= 4) | (i == 5 + c))
            def _():
                remote(xg.at[i, c], xg.at[later, c], ag_send.at[i, c], ag_recv.at[later, c], target).start()

        part = jnp.dot(xg[i, c], wq[...], preferred_element_type=F32).astype(BF)
        for h in range(NK):
            qp[c, i, h] = part[:, h * HD:(h + 1) * HD]
        remote(
            qp.at[c, i, pl.ds(2 - 2 * co, 2)], sib.at[c, i], sib_send.at[c, i], sib_recv.at[c, i], (sibling, p, t)
        ).start()

    def join_cores(c, i):
        @pl.when(i == 0)
        def _():
            await_bytes(cnt_two.at[c, co], c2_recv.at[c])
            for n in range(2):
                b = c * NK + 2 * co + n
                reach(cnt_two.at[c], cnt.at[zh], cnt_send.at[c], cnt_recv.at[0], (p, b, t), on_diag & (b == p))

        await_bytes(sib.at[c, i], sib_recv.at[c, i])
        for n in range(2):
            b = c * NK + 2 * co + n
            qs[c, i, n] = (qp[c, i, 2 * co + n].astype(F32) + sib[c, i, n].astype(F32)).astype(BF)
            reach(qs.at[c, i, n], qin.at[i, zh], qs_send.at[c, i], qin_recv.at[i], (p, b, t), on_diag & (b == p))

    def attend(c, i):
        @pl.when(i == 0)
        def _():
            await_bytes(cnt, cnt_recv.at[0])

        await_bytes(kvh.at[i, :, 0], kv_own.at[i])
        await_bytes(kvh.at[i, :, pl.ds(0, 3)], kv_recv.at[i])
        await_bytes(qin.at[i], qin_recv.at[i])
        total = qin[i, 0].astype(F32)
        for n in range(1, NK):
            total = total + qin[i, n].astype(F32)
        q = total.astype(BF)
        g = sequence_of(i)
        count = cnt[g // 2, g % 2][0:1, :]
        scores = []
        for n in range(NK):
            s = lax.dot_general(
                q, kvh[i, 0, n], (((1,), (1,)), ((), ())), preferred_element_type=F32
            ) * (1.0 / math.sqrt(HD))
            scores.append(jnp.where(count > n, s, NEG))
        top = jnp.max(
            jnp.maximum(jnp.maximum(scores[0], scores[1]), jnp.maximum(scores[2], scores[3])), axis=1, keepdims=True
        )
        e = [jnp.exp(s - top) for s in scores]
        den = jnp.sum((e[0] + e[1]) + (e[2] + e[3]), axis=1, keepdims=True)
        o = jnp.dot(e[0].astype(BF), kvh[i, 1, 0], preferred_element_type=F32)
        for n in range(1, NK):
            o = o + jnp.dot(e[n].astype(BF), kvh[i, 1, n], preferred_element_type=F32)
        att[i] = (o / den).astype(BF)
        for n in range(NK):
            dev = ((zh + n) % NK * 2 + k // 2, d, t)
            reach(
                att.at[i], ain.at[c_own, i, k], at_send.at[i], at_recv.at[c_own, i], dev,
                query_self & ((zh + n) % NK == zh),
            )

    def hand_over(c, i):
        pair = ain.at[c, i, pl.ds(2 * co, 2)]
        await_bytes(pair, at_recv.at[c, i])
        remote(pair, pair, fw_send.at[c, i], fw_recv.at[c, i], (sibling, p, t)).start()

    def mix(c, i):
        @pl.when((c == 0) & (i == 0))
        def _():
            loads[4].wait()

        await_bytes(ain.at[c, i, pl.ds(0, 2)], fw_recv.at[c, i])
        rows = jnp.concatenate([ain[c, i, h] for h in range(NK)], axis=1)
        pm[c, i] = jnp.dot(rows, wo[...], preferred_element_type=F32)

    def pass_on(c, slot, later, tensor_to, incoming):
        mine = pm[c, slot]
        if incoming:
            await_bytes(rin.at[c, slot], rs_recv.at[c, slot])
            mine = mine + rin[c, slot].astype(F32)
        rsb[c, slot] = mine.astype(BF)
        remote(
            rsb.at[c, slot], rin.at[c, later], rs_send.at[c, slot], rs_recv.at[c, later], (d, p, tensor_to)
        ).start()

    def ring(c, r):
        down = {1: (5, 3), 2: (3, 1), 3: (1, 0)}
        upward = {1: (6, 4), 2: (4, 2), 3: (2, 7)}
        if r == 0 and c == 0:
            pass_on(c, 7, 5, dn, False)
            pass_on(c, 6, 4, up, False)
        elif r == 0:
            pass_on(c, 7, 6, up, False)
            pass_on(c, 5, 3, dn, False)
        elif r == 1 and c == 0:
            pass_on(c, *down[r], dn, True)
        elif r == 1:
            pass_on(c, *upward[r], up, True)
        elif r < 4:
            pass_on(c, *down[r], dn, True)
            pass_on(c, *upward[r], up, True)
        else:
            await_bytes(rin.at[c, 0], rs_recv.at[c, 0])
            await_bytes(rin.at[c, 7], rs_recv.at[c, 7])
            out[c * 64:(c + 1) * 64] = (pm[c, 0] + rin[c, 0].astype(F32) + rin[c, 7].astype(F32)).astype(BF)

    stages = (
        (project, None), (join_cores, None), (attend, c_own), (hand_over, None), (mix, None),
    )

    def step(u, carry):
        for lag, (stage, only) in zip(LAGS, stages):
            v = u - lag
            c, i = (v // NG, v % NG) if BY_SPAN else (v % 2, v // 2)
            run = (v >= 0) & (v < UNITS)

            @pl.when(run if only is None else run & (c == only))
            def _():
                stage(c, i)

        for (c, r), at in RING_AT.items():
            @pl.when(u == at)
            def _():
                ring(c, r)

        return carry

    lax.fori_loop(0, UNITS + LAGS[-1], step, 0)
    for r in range(5):
        for c in range(2):
            if (c, r) not in RING_AT:
                ring(c, r)

    for way in range(2):
        for half in range(2):
            await_bytes(xg.at[0, half], own_send.at[way, half])
    for i in range(1, 7):
        for half in range(2):
            if i <= 4 or i == 5 + half:
                await_bytes(xg.at[i, half], ag_send.at[i, half])
    for c in range(2):
        await_bytes(cnt_two.at[c, co], c2_send.at[c])

    def drain(i, carry):
        for c in range(2):
            @pl.when(i >= 1)
            def _():
                await_bytes(rsb.at[c, i], rs_send.at[c, i])

            await_bytes(sib.at[c, i], sib_send.at[c, i])
            one_less = query_self & (c == c_own)

            @pl.when(one_less)
            def _():
                await_bytes(qs.at[c, i, 0], qs_send.at[c, i])

            @pl.when(jnp.logical_not(one_less))
            def _():
                await_bytes(qs.at[c, i], qs_send.at[c, i])

            @pl.when((i == 0) & one_less)
            def _():
                await_bytes(cnt.at[0], cnt_send.at[c])

            @pl.when((i == 0) & jnp.logical_not(one_less))
            def _():
                await_bytes(cnt.at[pl.ds(0, 2)], cnt_send.at[c])

        await_bytes(kvh.at[i, :, pl.ds(0, 3)], kv_send.at[i])

        @pl.when(query_self)
        def _():
            await_bytes(qin.at[i, pl.ds(0, 3)], at_send.at[i])

        @pl.when(jnp.logical_not(query_self))
        def _():
            await_bytes(qin.at[i], at_send.at[i])

        for c in range(2):
            await_bytes(ain.at[c, i, pl.ds(0, 2)], fw_send.at[c, i])
        return carry

    lax.fori_loop(0, NG, drain, 0)


def on_device(normed, w_query, neighbour_kv, counts, w_out):
    dma = pltpu.SemaphoreType.DMA
    anywhere = pl.BlockSpec(memory_space=pl.ANY)
    both = dma((2, NG))
    one = dma((NG,))
    return pl.pallas_call(
        kernel,
        out_shape=jax.ShapeDtypeStruct((128, 1024), BF),
        in_specs=[anywhere, anywhere, anywhere, pl.BlockSpec(memory_space=pltpu.SMEM), anywhere],
        out_specs=pl.BlockSpec(memory_space=pltpu.VMEM),
        scratch_shapes=[
            pltpu.VMEM((NG, 2, 64, 1024), BF),
            pltpu.VMEM((1024, 512), BF),
            pltpu.VMEM((NG, 2, 128, 512), BF),
            pltpu.VMEM((NG, 2, NK, 128, HD), BF),
            pltpu.VMEM((512, 1024), BF),
            pltpu.VMEM((2, NG, NK, 64, HD), BF),
            pltpu.VMEM((2, NG, 2, 64, HD), BF),
            pltpu.VMEM((2, NG, 2, 64, HD), BF),
            pltpu.VMEM((NG, NK, 64, HD), BF),
            pltpu.VMEM((NG, 64, HD), BF),
            pltpu.VMEM((2, NG, NK, 64, HD), BF),
            pltpu.VMEM((2, NG, 64, 1024), F32),
            pltpu.VMEM((2, NG, 64, 1024), BF),
            pltpu.VMEM((2, NG, 64, 1024), BF),
            pltpu.VMEM((2, 2, 8, 128), jnp.int32),
            pltpu.VMEM((NK, 2, 8, 128), jnp.int32),
            dma((5,)), dma((2, 2)), dma((NG, 2)), dma((NG, 2)),
            both, both, both, one, one, one, one,
            one, both, both, both, both, both, dma((2,)), dma((2,)), dma((2,)), dma((1,)),
        ],
        compiler_params=pltpu.CompilerParams(
            collective_id=0, has_side_effects=True, vmem_limit_bytes=60 * 1024 * 1024
        ),
        cost_estimate=pl.CostEstimate(flops=2_500_000_000, bytes_accessed=5_000_000, transcendentals=300_000),
    )(
        normed.reshape(2, 64, 1024),
        w_query.reshape(1024, 512),
        neighbour_kv.reshape(NG, 2, 128, 512),
        counts,
        w_out.reshape(512, 1024),
    )[None]


def solution(mesh):
    return jax.shard_map(
        on_device,
        mesh=mesh,
        in_specs=(
            P("pipe", "tensor", "dp"),
            P("pipe", "dp", "tensor"),
            P("dp", None, "pipe", None, None, "tensor"),
            P("pipe", "dp", None),
            P("pipe", "tensor", "dp"),
        ),
        out_specs=P("pipe", "tensor", "dp"),
        check_vma=False,
    )
```

```python
import math

import jax
import jax.numpy as jnp
from jax import lax
from jax.experimental import pallas as pl
from jax.experimental.pallas import tpu as pltpu
from jax.sharding import PartitionSpec as P

MESH = pl.DeviceIdType.MESH
BF = jnp.bfloat16
F32 = jnp.float32
HD = 128
NEG = -3.0e38
NG = 8
NK = 4
UNITS = 2 * NG
LAGS = (0, 2, 2, 6, 9, 11)
BY_SPAN = False
AHEAD = 2
FIRST = 1
RING_AT = {}


def kernel(
    normed, wq_in, kv_in, counts, wo_in, out,
    xg, wq, kv, kvh, via, wo, qp, sib, qs, qin, att, ain, pm, rsb, rin, cnt_two, cnt,
    ld_sem, own_send, ag_send, ag_recv, sib_send, sib_recv, qs_send, qin_recv, kv_own, kv_send, kv_recv, via_send, via_recv, on_send,
    at_send, at_recv, fw_send, fw_recv, rs_send, rs_recv, c2_send, c2_recv, cnt_send, cnt_recv,
):
    d = lax.axis_index("dp")
    p = lax.axis_index("pipe")
    t = lax.axis_index("tensor")
    zh = d // 2
    co = d % 2
    sibling = d + 1 - 2 * co
    c_own = p // NK
    k = p % NK
    up = (t + 1) % NG
    dn = (t + NG - 1) % NG
    on_diag = d == p
    query_self = on_diag & (k // 2 == co)

    def local(src, dst, sem):
        return pltpu.make_async_copy(src, dst, sem)

    def remote(src, dst, ssem, rsem, dev):
        return pltpu.make_async_remote_copy(
            src_ref=src, dst_ref=dst, send_sem=ssem, recv_sem=rsem, device_id=dev, device_id_type=MESH
        )

    def reach(src, dst, ssem, rsem, dev, is_self):
        @pl.when(is_self)
        def _():
            local(src, dst, rsem).start()

        @pl.when(jnp.logical_not(is_self))
        def _():
            remote(src, dst, ssem, rsem, dev).start()

    def await_bytes(ref, sem):
        local(ref, ref, sem).wait()

    loads = [
        local(normed.at[0], xg.at[0, 0], ld_sem.at[0]),
        local(normed.at[1], xg.at[0, 1], ld_sem.at[1]),
        local(wq_in, wq, ld_sem.at[2]),
        local(wo_in, wo, ld_sem.at[3]),
    ] + [local(kv_in.at[:, :, :, pl.ds(h * HD, HD)], kv.at[h], ld_sem.at[4 + h]) for h in range(NK)]
    for load in loads:
        load.start()

    barrier = pltpu.get_barrier_semaphore()

    def greet(dev):
        pl.semaphore_signal(barrier, inc=1, device_id=dev, device_id_type=MESH)

    def greet_other(dev, is_self):
        @pl.when(jnp.logical_not(is_self))
        def _():
            greet(dev)

    greet((d, p, up))
    greet((d, p, dn))
    for n in range(NK):
        b = (n % 2) * NK + 2 * co + n // 2
        greet_other((p, b, t), on_diag & (b == p))
        source = 2 * n + k // 2
        greet_other((source, d, t), on_diag & (source == d))
    for n in range(1, NK):
        greet((d, c_own * NK + (k + n) % NK, t))
    greet((sibling, p, t))
    for span in range(2):
        cnt_two[span, co] = jnp.full((8, 128), counts[0, 0, span], jnp.int32)
    pl.semaphore_wait(barrier, 14 - 2 * jnp.where(query_self, 1, 0))

    for half in range(2):
        loads[half].wait()
        remote(xg.at[0, half], xg.at[1, half], own_send.at[0, half], ag_recv.at[1, half], (d, p, up)).start()
        remote(xg.at[0, half], xg.at[2, half], own_send.at[1, half], ag_recv.at[2, half], (d, p, dn)).start()
    for span in range(2):
        remote(
            cnt_two.at[span, co], cnt_two.at[span, co], c2_send.at[span], c2_recv.at[span], (sibling, p, t)
        ).start()
    for h in range(NK):
        loads[4 + h].wait()

    def sequence_of(i):
        hop = (i + 1) // 2
        return (t + NG + jnp.where(i % 2 == 1, -hop, hop)) % NG

    def along_x(n):
        return (d, c_own * NK + (k + n) % NK, t)

    def send_heads(i, carry):
        g = sequence_of(i)
        local(kv.at[k, g], kvh.at[i, k], kv_own.at[i]).start()
        for n in (1, 3):
            remote(kv.at[(k + n) % NK, g], kvh.at[i, k], kv_send.at[i], kv_recv.at[i], along_x(n)).start()
        far = kv.at[(k + 2) % NK, g]

        @pl.when(i % 2 == 0)
        def _():
            remote(far, kvh.at[i, k], kv_send.at[i], kv_recv.at[i], along_x(2)).start()

        @pl.when(i % 2 == 1)
        def _():
            remote(far, via.at[i // 2], via_send.at[i // 2], via_recv.at[i // 2], along_x(FIRST)).start()

        return carry

    lax.fori_loop(0, AHEAD, send_heads, 0)
    loads[2].wait()

    def project(c, i):
        @pl.when(i >= 1)
        def _():
            await_bytes(xg.at[i, c], ag_recv.at[i, c])
            upward = i % 2 == 1
            target = (d, p, jnp.where(upward, up, dn))
            later = jnp.minimum(i + 2, NG - 1)

            @pl.when((i <= 4) | (i == 5 + c))
            def _():
                remote(xg.at[i, c], xg.at[later, c], ag_send.at[i, c], ag_recv.at[later, c], target).start()

        @pl.when((c == 0) & (i < NG - AHEAD))
        def _():
            send_heads(i + AHEAD, 0)

        part = jnp.dot(xg[i, c], wq[...], preferred_element_type=F32).astype(BF)
        for h in range(NK):
            qp[c, i, h] = part[:, h * HD:(h + 1) * HD]
        remote(
            qp.at[c, i, pl.ds(2 - 2 * co, 2)], sib.at[c, i], sib_send.at[c, i], sib_recv.at[c, i], (sibling, p, t)
        ).start()

    def join_cores(c, i):
        @pl.when(i == 0)
        def _():
            await_bytes(cnt_two.at[c, co], c2_recv.at[c])
            for n in range(2):
                b = c * NK + 2 * co + n
                reach(cnt_two.at[c], cnt.at[zh], cnt_send.at[c], cnt_recv.at[0], (p, b, t), on_diag & (b == p))

        await_bytes(sib.at[c, i], sib_recv.at[c, i])
        for n in range(2):
            b = c * NK + 2 * co + n
            qs[c, i, n] = (qp[c, i, 2 * co + n].astype(F32) + sib[c, i, n].astype(F32)).astype(BF)
            reach(qs.at[c, i, n], qin.at[i, zh], qs_send.at[c, i], qin_recv.at[i], (p, b, t), on_diag & (b == p))

    def relay(c, i):
        @pl.when(i % 2 == 1)
        def _():
            j = i // 2
            await_bytes(via.at[j], via_recv.at[j])
            remote(via.at[j], kvh.at[i, (k + NK - FIRST) % NK], on_send.at[j], kv_recv.at[i], along_x(FIRST)).start()

    def attend(c, i):
        @pl.when(i == 0)
        def _():
            await_bytes(cnt, cnt_recv.at[0])

        await_bytes(kvh.at[i, 0], kv_own.at[i])
        await_bytes(kvh.at[i, pl.ds(0, 3)], kv_recv.at[i])
        await_bytes(qin.at[i], qin_recv.at[i])
        total = qin[i, 0].astype(F32)
        for n in range(1, NK):
            total = total + qin[i, n].astype(F32)
        q = total.astype(BF)
        g = sequence_of(i)
        count = cnt[g // 2, g % 2][0:1, :]
        scores = []
        for n in range(NK):
            s = lax.dot_general(
                q, kvh[i, n, 0], (((1,), (1,)), ((), ())), preferred_element_type=F32
            ) * (1.0 / math.sqrt(HD))
            scores.append(jnp.where(count > n, s, NEG))
        top = jnp.max(
            jnp.maximum(jnp.maximum(scores[0], scores[1]), jnp.maximum(scores[2], scores[3])), axis=1, keepdims=True
        )
        e = [jnp.exp(s - top) for s in scores]
        den = jnp.sum((e[0] + e[1]) + (e[2] + e[3]), axis=1, keepdims=True)
        o = jnp.dot(e[0].astype(BF), kvh[i, 0, 1], preferred_element_type=F32)
        for n in range(1, NK):
            o = o + jnp.dot(e[n].astype(BF), kvh[i, n, 1], preferred_element_type=F32)
        att[i] = (o / den).astype(BF)
        for n in range(NK):
            dev = ((zh + n) % NK * 2 + k // 2, d, t)
            reach(
                att.at[i], ain.at[c_own, i, k], at_send.at[i], at_recv.at[c_own, i], dev,
                query_self & ((zh + n) % NK == zh),
            )

    def hand_over(c, i):
        pair = ain.at[c, i, pl.ds(2 * co, 2)]
        await_bytes(pair, at_recv.at[c, i])
        remote(pair, pair, fw_send.at[c, i], fw_recv.at[c, i], (sibling, p, t)).start()

    def mix(c, i):
        @pl.when((c == 0) & (i == 0))
        def _():
            loads[3].wait()

        await_bytes(ain.at[c, i, pl.ds(0, 2)], fw_recv.at[c, i])
        rows = jnp.concatenate([ain[c, i, h] for h in range(NK)], axis=1)
        pm[c, i] = jnp.dot(rows, wo[...], preferred_element_type=F32)

    def pass_on(c, slot, later, tensor_to, incoming):
        mine = pm[c, slot]
        if incoming:
            await_bytes(rin.at[c, slot], rs_recv.at[c, slot])
            mine = mine + rin[c, slot].astype(F32)
        rsb[c, slot] = mine.astype(BF)
        remote(
            rsb.at[c, slot], rin.at[c, later], rs_send.at[c, slot], rs_recv.at[c, later], (d, p, tensor_to)
        ).start()

    def ring(c, r):
        down = {1: (5, 3), 2: (3, 1), 3: (1, 0)}
        upward = {1: (6, 4), 2: (4, 2), 3: (2, 7)}
        if r == 0 and c == 0:
            pass_on(c, 7, 5, dn, False)
            pass_on(c, 6, 4, up, False)
        elif r == 0:
            pass_on(c, 7, 6, up, False)
            pass_on(c, 5, 3, dn, False)
        elif r == 1 and c == 0:
            pass_on(c, *down[r], dn, True)
        elif r == 1:
            pass_on(c, *upward[r], up, True)
        elif r < 4:
            pass_on(c, *down[r], dn, True)
            pass_on(c, *upward[r], up, True)
        else:
            await_bytes(rin.at[c, 0], rs_recv.at[c, 0])
            await_bytes(rin.at[c, 7], rs_recv.at[c, 7])
            out[c * 64:(c + 1) * 64] = (pm[c, 0] + rin[c, 0].astype(F32) + rin[c, 7].astype(F32)).astype(BF)

    stages = (
        (project, None), (join_cores, None), (relay, c_own), (attend, c_own), (hand_over, None), (mix, None),
    )

    def step(u, carry):
        for lag, (stage, only) in zip(LAGS, stages):
            v = u - lag
            c, i = (v // NG, v % NG) if BY_SPAN else (v % 2, v // 2)
            run = (v >= 0) & (v < UNITS)

            @pl.when(run if only is None else run & (c == only))
            def _():
                stage(c, i)

        for (c, r), at in RING_AT.items():
            @pl.when(u == at)
            def _():
                ring(c, r)

        return carry

    lax.fori_loop(0, UNITS + LAGS[-1], step, 0)
    for r in range(5):
        for c in range(2):
            if (c, r) not in RING_AT:
                ring(c, r)

    for way in range(2):
        for half in range(2):
            await_bytes(xg.at[0, half], own_send.at[way, half])
    for i in range(1, 7):
        for half in range(2):
            if i <= 4 or i == 5 + half:
                await_bytes(xg.at[i, half], ag_send.at[i, half])
    for c in range(2):
        await_bytes(cnt_two.at[c, co], c2_send.at[c])

    def drain(i, carry):
        for c in range(2):
            @pl.when(i >= 1)
            def _():
                await_bytes(rsb.at[c, i], rs_send.at[c, i])

            await_bytes(sib.at[c, i], sib_send.at[c, i])
            one_less = query_self & (c == c_own)

            @pl.when(one_less)
            def _():
                await_bytes(qs.at[c, i, 0], qs_send.at[c, i])

            @pl.when(jnp.logical_not(one_less))
            def _():
                await_bytes(qs.at[c, i], qs_send.at[c, i])

            @pl.when((i == 0) & one_less)
            def _():
                await_bytes(cnt.at[0], cnt_send.at[c])

            @pl.when((i == 0) & jnp.logical_not(one_less))
            def _():
                await_bytes(cnt.at[pl.ds(0, 2)], cnt_send.at[c])


        @pl.when(i % 2 == 0)
        def _():
            await_bytes(kvh.at[i, pl.ds(0, 3)], kv_send.at[i])

        @pl.when(i % 2 == 1)
        def _():
            await_bytes(kvh.at[i, pl.ds(0, 2)], kv_send.at[i])
            await_bytes(via.at[i // 2], via_send.at[i // 2])
            await_bytes(via.at[i // 2], on_send.at[i // 2])


        @pl.when(query_self)
        def _():
            await_bytes(qin.at[i, pl.ds(0, 3)], at_send.at[i])

        @pl.when(jnp.logical_not(query_self))
        def _():
            await_bytes(qin.at[i], at_send.at[i])

        for c in range(2):
            await_bytes(ain.at[c, i, pl.ds(0, 2)], fw_send.at[c, i])
        return carry

    lax.fori_loop(0, NG, drain, 0)


def on_device(normed, w_query, neighbour_kv, counts, w_out):
    dma = pltpu.SemaphoreType.DMA
    anywhere = pl.BlockSpec(memory_space=pl.ANY)
    both = dma((2, NG))
    one = dma((NG,))
    return pl.pallas_call(
        kernel,
        out_shape=jax.ShapeDtypeStruct((128, 1024), BF),
        in_specs=[anywhere, anywhere, anywhere, pl.BlockSpec(memory_space=pltpu.SMEM), anywhere],
        out_specs=pl.BlockSpec(memory_space=pltpu.VMEM),
        scratch_shapes=[
            pltpu.VMEM((NG, 2, 64, 1024), BF),
            pltpu.VMEM((1024, 512), BF),
            pltpu.VMEM((NK, NG, 2, 128, HD), BF),
            pltpu.VMEM((NG, NK, 2, 128, HD), BF),
            pltpu.VMEM((NG // 2, 2, 128, HD), BF),
            pltpu.VMEM((512, 1024), BF),
            pltpu.VMEM((2, NG, NK, 64, HD), BF),
            pltpu.VMEM((2, NG, 2, 64, HD), BF),
            pltpu.VMEM((2, NG, 2, 64, HD), BF),
            pltpu.VMEM((NG, NK, 64, HD), BF),
            pltpu.VMEM((NG, 64, HD), BF),
            pltpu.VMEM((2, NG, NK, 64, HD), BF),
            pltpu.VMEM((2, NG, 64, 1024), F32),
            pltpu.VMEM((2, NG, 64, 1024), BF),
            pltpu.VMEM((2, NG, 64, 1024), BF),
            pltpu.VMEM((2, 2, 8, 128), jnp.int32),
            pltpu.VMEM((NK, 2, 8, 128), jnp.int32),
            dma((8,)), dma((2, 2)), dma((NG, 2)), dma((NG, 2)),
            both, both, both, one, one, one, one,
            dma((NG // 2,)), dma((NG // 2,)), dma((NG // 2,)), one, both, both, both, both, both, dma((2,)), dma((2,)), dma((2,)), dma((1,)),
        ],
        compiler_params=pltpu.CompilerParams(
            collective_id=0, has_side_effects=True, vmem_limit_bytes=60 * 1024 * 1024
        ),
        cost_estimate=pl.CostEstimate(flops=2_500_000_000, bytes_accessed=5_000_000, transcendentals=300_000),
    )(
        normed.reshape(2, 64, 1024),
        w_query.reshape(1024, 512),
        neighbour_kv.reshape(NG, 2, 128, 512),
        counts,
        w_out.reshape(512, 1024),
    )[None]


def solution(mesh):
    return jax.shard_map(
        on_device,
        mesh=mesh,
        in_specs=(
            P("pipe", "tensor", "dp"),
            P("pipe", "dp", "tensor"),
            P("dp", None, "pipe", None, None, "tensor"),
            P("pipe", "dp", None),
            P("pipe", "tensor", "dp"),
        ),
        out_specs=P("pipe", "tensor", "dp"),
        check_vma=False,
    )
```

```python
import math

import jax
import jax.numpy as jnp
from jax import lax
from jax.experimental import pallas as pl
from jax.experimental.pallas import tpu as pltpu
from jax.sharding import PartitionSpec as P

MESH = pl.DeviceIdType.MESH
BF = jnp.bfloat16
F32 = jnp.float32
HD = 128
NEG = -3.0e38
NG = 8
NK = 4
UNITS = 2 * NG
LAGS = (0, 2, 2, 6, 9, 11)
BY_SPAN = False
STAG_AG = True
STAG_RS = True
AHEAD = 2
FIRST = 1
RING_AT = {}


def kernel(
    normed, wq_in, kv_in, counts, wo_in, out,
    xg, wq, kv, kvh, via, wo, qp, sib, qs, qin, att, ain, pm, rsb, rin, cnt_two, cnt,
    ld_sem, own_send, ag_send, ag_recv, sib_send, sib_recv, qs_send, qin_recv, kv_own, kv_send, kv_recv, via_send, via_recv, on_send,
    at_send, at_recv, fw_send, fw_recv, rs_send, rs_recv, c2_send, c2_recv, cnt_send, cnt_recv,
):
    d = lax.axis_index("dp")
    p = lax.axis_index("pipe")
    t = lax.axis_index("tensor")
    zh = d // 2
    co = d % 2
    sibling = d + 1 - 2 * co
    c_own = p // NK
    k = p % NK
    up = (t + 1) % NG
    dn = (t + NG - 1) % NG
    on_diag = d == p
    query_self = on_diag & (k // 2 == co)

    def local(src, dst, sem):
        return pltpu.make_async_copy(src, dst, sem)

    def remote(src, dst, ssem, rsem, dev):
        return pltpu.make_async_remote_copy(
            src_ref=src, dst_ref=dst, send_sem=ssem, recv_sem=rsem, device_id=dev, device_id_type=MESH
        )

    def reach(src, dst, ssem, rsem, dev, is_self):
        @pl.when(is_self)
        def _():
            local(src, dst, rsem).start()

        @pl.when(jnp.logical_not(is_self))
        def _():
            remote(src, dst, ssem, rsem, dev).start()

    def await_bytes(ref, sem):
        local(ref, ref, sem).wait()

    loads = [
        local(normed.at[0], xg.at[0, 0], ld_sem.at[0]),
        local(normed.at[1], xg.at[0, 1], ld_sem.at[1]),
        local(wq_in, wq, ld_sem.at[2]),
        local(wo_in, wo, ld_sem.at[3]),
    ] + [local(kv_in.at[:, :, :, pl.ds(h * HD, HD)], kv.at[h], ld_sem.at[4 + h]) for h in range(NK)]
    for load in loads:
        load.start()

    barrier = pltpu.get_barrier_semaphore()

    def greet(dev):
        pl.semaphore_signal(barrier, inc=1, device_id=dev, device_id_type=MESH)

    def greet_other(dev, is_self):
        @pl.when(jnp.logical_not(is_self))
        def _():
            greet(dev)

    greet((d, p, up))
    greet((d, p, dn))
    for n in range(NK):
        b = (n % 2) * NK + 2 * co + n // 2
        greet_other((p, b, t), on_diag & (b == p))
        source = 2 * n + k // 2
        greet_other((source, d, t), on_diag & (source == d))
    for n in range(1, NK):
        greet((d, c_own * NK + (k + n) % NK, t))
    greet((sibling, p, t))
    for span in range(2):
        cnt_two[span, co] = jnp.full((8, 128), counts[0, 0, span], jnp.int32)
    pl.semaphore_wait(barrier, 14 - 2 * jnp.where(query_self, 1, 0))

    def send_own(half):
        loads[half].wait()
        remote(xg.at[0, half], xg.at[1, half], own_send.at[0, half], ag_recv.at[1, half], (d, p, up)).start()
        remote(xg.at[0, half], xg.at[2, half], own_send.at[1, half], ag_recv.at[2, half], (d, p, dn)).start()

    send_own(0)
    if not STAG_AG:
        send_own(1)
    for span in range(2):
        remote(
            cnt_two.at[span, co], cnt_two.at[span, co], c2_send.at[span], c2_recv.at[span], (sibling, p, t)
        ).start()
    for h in range(NK):
        loads[4 + h].wait()

    def sequence_of(i):
        hop = (i + 1) // 2
        return (t + NG + jnp.where(i % 2 == 1, -hop, hop)) % NG

    def along_x(n):
        return (d, c_own * NK + (k + n) % NK, t)

    def send_heads(i, carry):
        g = sequence_of(i)
        local(kv.at[k, g], kvh.at[i, k], kv_own.at[i]).start()
        for n in (1, 3):
            remote(kv.at[(k + n) % NK, g], kvh.at[i, k], kv_send.at[i], kv_recv.at[i], along_x(n)).start()
        far = kv.at[(k + 2) % NK, g]

        @pl.when(i % 2 == 0)
        def _():
            remote(far, kvh.at[i, k], kv_send.at[i], kv_recv.at[i], along_x(2)).start()

        @pl.when(i % 2 == 1)
        def _():
            remote(far, via.at[i // 2], via_send.at[i // 2], via_recv.at[i // 2], along_x(FIRST)).start()

        return carry

    lax.fori_loop(0, AHEAD, send_heads, 0)
    if STAG_AG:
        for way in range(2):
            await_bytes(xg.at[0, 0], own_send.at[way, 0])
        send_own(1)
    loads[2].wait()

    def project(c, i):
        @pl.when(i >= 1)
        def _():
            await_bytes(xg.at[i, c], ag_recv.at[i, c])
            upward = i % 2 == 1
            target = (d, p, jnp.where(upward, up, dn))
            later = jnp.minimum(i + 2, NG - 1)

            @pl.when((i <= 4) | (i == 5 + c))
            def _():
                remote(xg.at[i, c], xg.at[later, c], ag_send.at[i, c], ag_recv.at[later, c], target).start()

        @pl.when((c == 0) & (i < NG - AHEAD))
        def _():
            send_heads(i + AHEAD, 0)

        part = jnp.dot(xg[i, c], wq[...], preferred_element_type=F32).astype(BF)
        for h in range(NK):
            qp[c, i, h] = part[:, h * HD:(h + 1) * HD]
        remote(
            qp.at[c, i, pl.ds(2 - 2 * co, 2)], sib.at[c, i], sib_send.at[c, i], sib_recv.at[c, i], (sibling, p, t)
        ).start()

    def join_cores(c, i):
        @pl.when(i == 0)
        def _():
            await_bytes(cnt_two.at[c, co], c2_recv.at[c])
            for n in range(2):
                b = c * NK + 2 * co + n
                reach(cnt_two.at[c], cnt.at[zh], cnt_send.at[c], cnt_recv.at[0], (p, b, t), on_diag & (b == p))

        await_bytes(sib.at[c, i], sib_recv.at[c, i])
        for n in range(2):
            b = c * NK + 2 * co + n
            qs[c, i, n] = (qp[c, i, 2 * co + n].astype(F32) + sib[c, i, n].astype(F32)).astype(BF)
            reach(qs.at[c, i, n], qin.at[i, zh], qs_send.at[c, i], qin_recv.at[i], (p, b, t), on_diag & (b == p))

    def relay(c, i):
        @pl.when(i % 2 == 1)
        def _():
            j = i // 2
            await_bytes(via.at[j], via_recv.at[j])
            remote(via.at[j], kvh.at[i, (k + NK - FIRST) % NK], on_send.at[j], kv_recv.at[i], along_x(FIRST)).start()

    def attend(c, i):
        @pl.when(i == 0)
        def _():
            await_bytes(cnt, cnt_recv.at[0])

        await_bytes(kvh.at[i, 0], kv_own.at[i])
        await_bytes(kvh.at[i, pl.ds(0, 3)], kv_recv.at[i])
        await_bytes(qin.at[i], qin_recv.at[i])
        total = qin[i, 0].astype(F32)
        for n in range(1, NK):
            total = total + qin[i, n].astype(F32)
        q = total.astype(BF)
        g = sequence_of(i)
        count = cnt[g // 2, g % 2][0:1, :]
        scores = []
        for n in range(NK):
            s = lax.dot_general(
                q, kvh[i, n, 0], (((1,), (1,)), ((), ())), preferred_element_type=F32
            ) * (1.0 / math.sqrt(HD))
            scores.append(jnp.where(count > n, s, NEG))
        top = jnp.max(
            jnp.maximum(jnp.maximum(scores[0], scores[1]), jnp.maximum(scores[2], scores[3])), axis=1, keepdims=True
        )
        e = [jnp.exp(s - top) for s in scores]
        den = jnp.sum((e[0] + e[1]) + (e[2] + e[3]), axis=1, keepdims=True)
        o = jnp.dot(e[0].astype(BF), kvh[i, 0, 1], preferred_element_type=F32)
        for n in range(1, NK):
            o = o + jnp.dot(e[n].astype(BF), kvh[i, n, 1], preferred_element_type=F32)
        att[i] = (o / den).astype(BF)
        for n in range(NK):
            dev = ((zh + n) % NK * 2 + k // 2, d, t)
            reach(
                att.at[i], ain.at[c_own, i, k], at_send.at[i], at_recv.at[c_own, i], dev,
                query_self & ((zh + n) % NK == zh),
            )

    def hand_over(c, i):
        pair = ain.at[c, i, pl.ds(2 * co, 2)]
        await_bytes(pair, at_recv.at[c, i])
        remote(pair, pair, fw_send.at[c, i], fw_recv.at[c, i], (sibling, p, t)).start()

    def mix(c, i):
        @pl.when((c == 0) & (i == 0))
        def _():
            loads[3].wait()

        await_bytes(ain.at[c, i, pl.ds(0, 2)], fw_recv.at[c, i])
        rows = jnp.concatenate([ain[c, i, h] for h in range(NK)], axis=1)
        pm[c, i] = jnp.dot(rows, wo[...], preferred_element_type=F32)

    def pass_on(c, slot, later, tensor_to, incoming):
        mine = pm[c, slot]
        if incoming:
            await_bytes(rin.at[c, slot], rs_recv.at[c, slot])
            mine = mine + rin[c, slot].astype(F32)
        rsb[c, slot] = mine.astype(BF)
        remote(
            rsb.at[c, slot], rin.at[c, later], rs_send.at[c, slot], rs_recv.at[c, later], (d, p, tensor_to)
        ).start()

    def ring(c, r):
        down = {1: (5, 3), 2: (3, 1), 3: (1, 0)}
        upward = {1: (6, 4), 2: (4, 2), 3: (2, 7)}
        if r == 0 and c == 0:
            pass_on(c, 7, 5, dn, False)
            pass_on(c, 6, 4, up, False)
            if STAG_RS:
                for slot in (7, 6):
                    await_bytes(rsb.at[c, slot], rs_send.at[c, slot])
        elif r == 0:
            pass_on(c, 7, 6, up, False)
            pass_on(c, 5, 3, dn, False)
        elif r == 1 and c == 0:
            pass_on(c, *down[r], dn, True)
        elif r == 1:
            pass_on(c, *upward[r], up, True)
        elif r < 4:
            pass_on(c, *down[r], dn, True)
            pass_on(c, *upward[r], up, True)
        else:
            await_bytes(rin.at[c, 0], rs_recv.at[c, 0])
            await_bytes(rin.at[c, 7], rs_recv.at[c, 7])
            out[c * 64:(c + 1) * 64] = (pm[c, 0] + rin[c, 0].astype(F32) + rin[c, 7].astype(F32)).astype(BF)

    stages = (
        (project, None), (join_cores, None), (relay, c_own), (attend, c_own), (hand_over, None), (mix, None),
    )

    def step(u, carry):
        for lag, (stage, only) in zip(LAGS, stages):
            v = u - lag
            c, i = (v // NG, v % NG) if BY_SPAN else (v % 2, v // 2)
            run = (v >= 0) & (v < UNITS)

            @pl.when(run if only is None else run & (c == only))
            def _():
                stage(c, i)

        for (c, r), at in RING_AT.items():
            @pl.when(u == at)
            def _():
                ring(c, r)

        return carry

    lax.fori_loop(0, UNITS + LAGS[-1], step, 0)
    for r in range(5):
        for c in range(2):
            if (c, r) not in RING_AT:
                ring(c, r)

    for way in range(2):
        for half in range(1 if STAG_AG else 0, 2):
            await_bytes(xg.at[0, half], own_send.at[way, half])
    for i in range(1, 7):
        for half in range(2):
            if i <= 4 or i == 5 + half:
                await_bytes(xg.at[i, half], ag_send.at[i, half])
    for c in range(2):
        await_bytes(cnt_two.at[c, co], c2_send.at[c])

    def drain(i, carry):
        for c in range(2):
            @pl.when((i >= 1) & (i < 6) if STAG_RS and c == 0 else (i >= 1))
            def _():
                await_bytes(rsb.at[c, i], rs_send.at[c, i])

            await_bytes(sib.at[c, i], sib_send.at[c, i])
            one_less = query_self & (c == c_own)

            @pl.when(one_less)
            def _():
                await_bytes(qs.at[c, i, 0], qs_send.at[c, i])

            @pl.when(jnp.logical_not(one_less))
            def _():
                await_bytes(qs.at[c, i], qs_send.at[c, i])

            @pl.when((i == 0) & one_less)
            def _():
                await_bytes(cnt.at[0], cnt_send.at[c])

            @pl.when((i == 0) & jnp.logical_not(one_less))
            def _():
                await_bytes(cnt.at[pl.ds(0, 2)], cnt_send.at[c])


        @pl.when(i % 2 == 0)
        def _():
            await_bytes(kvh.at[i, pl.ds(0, 3)], kv_send.at[i])

        @pl.when(i % 2 == 1)
        def _():
            await_bytes(kvh.at[i, pl.ds(0, 2)], kv_send.at[i])
            await_bytes(via.at[i // 2], via_send.at[i // 2])
            await_bytes(via.at[i // 2], on_send.at[i // 2])


        @pl.when(query_self)
        def _():
            await_bytes(qin.at[i, pl.ds(0, 3)], at_send.at[i])

        @pl.when(jnp.logical_not(query_self))
        def _():
            await_bytes(qin.at[i], at_send.at[i])

        for c in range(2):
            await_bytes(ain.at[c, i, pl.ds(0, 2)], fw_send.at[c, i])
        return carry

    lax.fori_loop(0, NG, drain, 0)


def on_device(normed, w_query, neighbour_kv, counts, w_out):
    dma = pltpu.SemaphoreType.DMA
    anywhere = pl.BlockSpec(memory_space=pl.ANY)
    both = dma((2, NG))
    one = dma((NG,))
    return pl.pallas_call(
        kernel,
        out_shape=jax.ShapeDtypeStruct((128, 1024), BF),
        in_specs=[anywhere, anywhere, anywhere, pl.BlockSpec(memory_space=pltpu.SMEM), anywhere],
        out_specs=pl.BlockSpec(memory_space=pltpu.VMEM),
        scratch_shapes=[
            pltpu.VMEM((NG, 2, 64, 1024), BF),
            pltpu.VMEM((1024, 512), BF),
            pltpu.VMEM((NK, NG, 2, 128, HD), BF),
            pltpu.VMEM((NG, NK, 2, 128, HD), BF),
            pltpu.VMEM((NG // 2, 2, 128, HD), BF),
            pltpu.VMEM((512, 1024), BF),
            pltpu.VMEM((2, NG, NK, 64, HD), BF),
            pltpu.VMEM((2, NG, 2, 64, HD), BF),
            pltpu.VMEM((2, NG, 2, 64, HD), BF),
            pltpu.VMEM((NG, NK, 64, HD), BF),
            pltpu.VMEM((NG, 64, HD), BF),
            pltpu.VMEM((2, NG, NK, 64, HD), BF),
            pltpu.VMEM((2, NG, 64, 1024), F32),
            pltpu.VMEM((2, NG, 64, 1024), BF),
            pltpu.VMEM((2, NG, 64, 1024), BF),
            pltpu.VMEM((2, 2, 8, 128), jnp.int32),
            pltpu.VMEM((NK, 2, 8, 128), jnp.int32),
            dma((8,)), dma((2, 2)), dma((NG, 2)), dma((NG, 2)),
            both, both, both, one, one, one, one,
            dma((NG // 2,)), dma((NG // 2,)), dma((NG // 2,)), one, both, both, both, both, both, dma((2,)), dma((2,)), dma((2,)), dma((1,)),
        ],
        compiler_params=pltpu.CompilerParams(
            collective_id=0, has_side_effects=True, vmem_limit_bytes=60 * 1024 * 1024
        ),
        cost_estimate=pl.CostEstimate(flops=2_500_000_000, bytes_accessed=5_000_000, transcendentals=300_000),
    )(
        normed.reshape(2, 64, 1024),
        w_query.reshape(1024, 512),
        neighbour_kv.reshape(NG, 2, 128, 512),
        counts,
        w_out.reshape(512, 1024),
    )[None]


def solution(mesh):
    return jax.shard_map(
        on_device,
        mesh=mesh,
        in_specs=(
            P("pipe", "tensor", "dp"),
            P("pipe", "dp", "tensor"),
            P("dp", None, "pipe", None, None, "tensor"),
            P("pipe", "dp", None),
            P("pipe", "tensor", "dp"),
        ),
        out_specs=P("pipe", "tensor", "dp"),
        check_vma=False,
    )
```

```python
import math

import jax
import jax.numpy as jnp
from jax import lax
from jax.experimental import pallas as pl
from jax.experimental.pallas import tpu as pltpu
from jax.sharding import PartitionSpec as P

MESH = pl.DeviceIdType.MESH
BF = jnp.bfloat16
F32 = jnp.float32
HD = 128
NEG = -3.0e38
NG = 8
NK = 4
UNITS = 2 * NG
LAGS = (0, 2, 6, 9, 11)
BY_SPAN = False
STAG_AG = True
STAG_RS = True
AHEAD = 2
RING_AT = {}


def kernel(
    normed, wq_in, kv_in, counts, wo_in, out,
    xg, wq, kv, kvh, wo, qp, sib, qs, qin, att, ain, pm, rsb, rin, cnt_two, cnt,
    ld_sem, own_send, ag_send, ag_recv, sib_send, sib_recv, qs_send, qin_recv, kv_own, kv_send, kv_recv,
    at_send, at_recv, fw_send, fw_recv, rs_send, rs_recv, c2_send, c2_recv, cnt_send, cnt_recv,
):
    d = lax.axis_index("dp")
    p = lax.axis_index("pipe")
    t = lax.axis_index("tensor")
    zh = d // 2
    co = d % 2
    sibling = d + 1 - 2 * co
    c_own = p // NK
    k = p % NK
    up = (t + 1) % NG
    dn = (t + NG - 1) % NG
    on_diag = d == p
    query_self = on_diag & (k // 2 == co)

    def local(src, dst, sem):
        return pltpu.make_async_copy(src, dst, sem)

    def remote(src, dst, ssem, rsem, dev):
        return pltpu.make_async_remote_copy(
            src_ref=src, dst_ref=dst, send_sem=ssem, recv_sem=rsem, device_id=dev, device_id_type=MESH
        )

    def reach(src, dst, ssem, rsem, dev, is_self):
        @pl.when(is_self)
        def _():
            local(src, dst, rsem).start()

        @pl.when(jnp.logical_not(is_self))
        def _():
            remote(src, dst, ssem, rsem, dev).start()

    def await_bytes(ref, sem):
        local(ref, ref, sem).wait()

    loads = [
        local(normed.at[0], xg.at[0, 0], ld_sem.at[0]),
        local(normed.at[1], xg.at[0, 1], ld_sem.at[1]),
        local(wq_in, wq, ld_sem.at[2]),
        local(wo_in, wo, ld_sem.at[3]),
    ] + [local(kv_in.at[:, :, :, pl.ds(h * HD, HD)], kv.at[h], ld_sem.at[4 + h]) for h in range(NK)]
    for load in loads:
        load.start()

    barrier = pltpu.get_barrier_semaphore()

    def greet(dev):
        pl.semaphore_signal(barrier, inc=1, device_id=dev, device_id_type=MESH)

    def greet_other(dev, is_self):
        @pl.when(jnp.logical_not(is_self))
        def _():
            greet(dev)

    for n in range(NK):
        b = (n % 2) * NK + 2 * co + n // 2
        greet_other((p, b, t), on_diag & (b == p))
        source = 2 * n + k // 2
        greet_other((source, d, t), on_diag & (source == d))
    for n in range(1, NK):
        greet((d, c_own * NK + (k + n) % NK, t))
    greet((d, p, up))
    greet((d, p, dn))
    greet((sibling, p, t))
    for span in range(2):
        cnt_two[span, co] = jnp.full((8, 128), counts[0, 0, span], jnp.int32)
    pl.semaphore_wait(barrier, 14 - 2 * jnp.where(query_self, 1, 0))

    def send_own(half):
        loads[half].wait()
        remote(xg.at[0, half], xg.at[1, half], own_send.at[0, half], ag_recv.at[1, half], (d, p, up)).start()
        remote(xg.at[0, half], xg.at[2, half], own_send.at[1, half], ag_recv.at[2, half], (d, p, dn)).start()

    send_own(0)
    if not STAG_AG:
        send_own(1)
    for span in range(2):
        remote(
            cnt_two.at[span, co], cnt_two.at[span, co], c2_send.at[span], c2_recv.at[span], (sibling, p, t)
        ).start()
    for h in range(NK):
        loads[4 + h].wait()

    def sequence_of(i):
        hop = (i + 1) // 2
        return (t + NG + jnp.where(i % 2 == 1, -hop, hop)) % NG

    def along_x(n):
        return (d, c_own * NK + (k + n) % NK, t)

    def send_heads(i, carry):
        g = sequence_of(i)
        local(kv.at[k, g], kvh.at[i, k], kv_own.at[i]).start()
        for n in (1, 3, 2):
            remote(kv.at[(k + n) % NK, g], kvh.at[i, k], kv_send.at[i], kv_recv.at[i], along_x(n)).start()
        return carry

    lax.fori_loop(0, AHEAD, send_heads, 0)
    if STAG_AG:
        for way in range(2):
            await_bytes(xg.at[0, 0], own_send.at[way, 0])
        send_own(1)
    loads[2].wait()

    def project(c, i):
        @pl.when(i >= 1)
        def _():
            await_bytes(xg.at[i, c], ag_recv.at[i, c])
            upward = i % 2 == 1
            target = (d, p, jnp.where(upward, up, dn))
            later = jnp.minimum(i + 2, NG - 1)

            @pl.when((i <= 4) | (i == 5 + c))
            def _():
                remote(xg.at[i, c], xg.at[later, c], ag_send.at[i, c], ag_recv.at[later, c], target).start()

        @pl.when((c == 0) & (i < NG - AHEAD))
        def _():
            send_heads(i + AHEAD, 0)

        part = jnp.dot(xg[i, c], wq[...], preferred_element_type=F32).astype(BF)
        for h in range(NK):
            qp[c, i, h] = part[:, h * HD:(h + 1) * HD]
        remote(
            qp.at[c, i, pl.ds(2 - 2 * co, 2)], sib.at[c, i], sib_send.at[c, i], sib_recv.at[c, i], (sibling, p, t)
        ).start()

    def join_cores(c, i):
        @pl.when(i == 0)
        def _():
            await_bytes(cnt_two.at[c, co], c2_recv.at[c])
            for n in range(2):
                b = c * NK + 2 * co + n
                reach(cnt_two.at[c], cnt.at[zh], cnt_send.at[c], cnt_recv.at[0], (p, b, t), on_diag & (b == p))

        await_bytes(sib.at[c, i], sib_recv.at[c, i])
        for n in range(2):
            b = c * NK + 2 * co + n
            qs[c, i, n] = (qp[c, i, 2 * co + n].astype(F32) + sib[c, i, n].astype(F32)).astype(BF)
            reach(qs.at[c, i, n], qin.at[i, zh], qs_send.at[c, i], qin_recv.at[i], (p, b, t), on_diag & (b == p))

    def attend(c, i):
        @pl.when(i == 0)
        def _():
            await_bytes(cnt, cnt_recv.at[0])

        await_bytes(kvh.at[i, 0], kv_own.at[i])
        await_bytes(kvh.at[i, pl.ds(0, 3)], kv_recv.at[i])
        await_bytes(qin.at[i], qin_recv.at[i])
        total = qin[i, 0].astype(F32)
        for n in range(1, NK):
            total = total + qin[i, n].astype(F32)
        q = total.astype(BF)
        g = sequence_of(i)
        count = cnt[g // 2, g % 2][0:1, :]
        scores = []
        for n in range(NK):
            s = lax.dot_general(
                q, kvh[i, n, 0], (((1,), (1,)), ((), ())), preferred_element_type=F32
            ) * (1.0 / math.sqrt(HD))
            scores.append(jnp.where(count > n, s, NEG))
        top = jnp.max(
            jnp.maximum(jnp.maximum(scores[0], scores[1]), jnp.maximum(scores[2], scores[3])), axis=1, keepdims=True
        )
        e = [jnp.exp(s - top) for s in scores]
        den = jnp.sum((e[0] + e[1]) + (e[2] + e[3]), axis=1, keepdims=True)
        o = jnp.dot(e[0].astype(BF), kvh[i, 0, 1], preferred_element_type=F32)
        for n in range(1, NK):
            o = o + jnp.dot(e[n].astype(BF), kvh[i, n, 1], preferred_element_type=F32)
        att[i] = (o / den).astype(BF)
        for n in range(NK):
            dev = ((zh + n) % NK * 2 + k // 2, d, t)
            reach(
                att.at[i], ain.at[c_own, i, k], at_send.at[i], at_recv.at[c_own, i], dev,
                query_self & ((zh + n) % NK == zh),
            )

    def hand_over(c, i):
        pair = ain.at[c, i, pl.ds(2 * co, 2)]
        await_bytes(pair, at_recv.at[c, i])
        remote(pair, pair, fw_send.at[c, i], fw_recv.at[c, i], (sibling, p, t)).start()

    def mix(c, i):
        @pl.when((c == 0) & (i == 0))
        def _():
            loads[3].wait()

        await_bytes(ain.at[c, i, pl.ds(0, 2)], fw_recv.at[c, i])
        rows = jnp.concatenate([ain[c, i, h] for h in range(NK)], axis=1)
        pm[c, i] = jnp.dot(rows, wo[...], preferred_element_type=F32)

    def pass_on(c, slot, later, tensor_to, incoming):
        mine = pm[c, slot]
        if incoming:
            await_bytes(rin.at[c, slot], rs_recv.at[c, slot])
            mine = mine + rin[c, slot].astype(F32)
        rsb[c, slot] = mine.astype(BF)
        remote(
            rsb.at[c, slot], rin.at[c, later], rs_send.at[c, slot], rs_recv.at[c, later], (d, p, tensor_to)
        ).start()

    def ring(c, r):
        down = {1: (5, 3), 2: (3, 1), 3: (1, 0)}
        upward = {1: (6, 4), 2: (4, 2), 3: (2, 7)}
        if r == 0 and c == 0:
            pass_on(c, 7, 5, dn, False)
            pass_on(c, 6, 4, up, False)
            if STAG_RS:
                for slot in (7, 6):
                    await_bytes(rsb.at[c, slot], rs_send.at[c, slot])
        elif r == 0:
            pass_on(c, 7, 6, up, False)
            pass_on(c, 5, 3, dn, False)
        elif r == 1 and c == 0:
            pass_on(c, *down[r], dn, True)
        elif r == 1:
            pass_on(c, *upward[r], up, True)
        elif r < 4:
            pass_on(c, *down[r], dn, True)
            pass_on(c, *upward[r], up, True)
        else:
            await_bytes(rin.at[c, 0], rs_recv.at[c, 0])
            await_bytes(rin.at[c, 7], rs_recv.at[c, 7])
            out[c * 64:(c + 1) * 64] = (pm[c, 0] + rin[c, 0].astype(F32) + rin[c, 7].astype(F32)).astype(BF)

    stages = (
        (project, None), (join_cores, None), (attend, c_own), (hand_over, None), (mix, None),
    )

    def step(u, carry):
        for lag, (stage, only) in zip(LAGS, stages):
            v = u - lag
            c, i = (v // NG, v % NG) if BY_SPAN else (v % 2, v // 2)
            run = (v >= 0) & (v < UNITS)

            @pl.when(run if only is None else run & (c == only))
            def _():
                stage(c, i)

        for (c, r), at in RING_AT.items():
            @pl.when(u == at)
            def _():
                ring(c, r)

        return carry

    lax.fori_loop(0, UNITS + LAGS[-1], step, 0)
    for r in range(5):
        for c in range(2):
            if (c, r) not in RING_AT:
                ring(c, r)

    for way in range(2):
        for half in range(1 if STAG_AG else 0, 2):
            await_bytes(xg.at[0, half], own_send.at[way, half])
    for i in range(1, 7):
        for half in range(2):
            if i <= 4 or i == 5 + half:
                await_bytes(xg.at[i, half], ag_send.at[i, half])
    for c in range(2):
        await_bytes(cnt_two.at[c, co], c2_send.at[c])

    def drain(i, carry):
        for c in range(2):
            @pl.when((i >= 1) & (i < 6) if STAG_RS and c == 0 else (i >= 1))
            def _():
                await_bytes(rsb.at[c, i], rs_send.at[c, i])

            await_bytes(sib.at[c, i], sib_send.at[c, i])
            one_less = query_self & (c == c_own)

            @pl.when(one_less)
            def _():
                await_bytes(qs.at[c, i, 0], qs_send.at[c, i])

            @pl.when(jnp.logical_not(one_less))
            def _():
                await_bytes(qs.at[c, i], qs_send.at[c, i])

            @pl.when((i == 0) & one_less)
            def _():
                await_bytes(cnt.at[0], cnt_send.at[c])

            @pl.when((i == 0) & jnp.logical_not(one_less))
            def _():
                await_bytes(cnt.at[pl.ds(0, 2)], cnt_send.at[c])

        await_bytes(kvh.at[i, pl.ds(0, 3)], kv_send.at[i])

        @pl.when(query_self)
        def _():
            await_bytes(qin.at[i, pl.ds(0, 3)], at_send.at[i])

        @pl.when(jnp.logical_not(query_self))
        def _():
            await_bytes(qin.at[i], at_send.at[i])

        for c in range(2):
            await_bytes(ain.at[c, i, pl.ds(0, 2)], fw_send.at[c, i])
        return carry

    lax.fori_loop(0, NG, drain, 0)


def on_device(normed, w_query, neighbour_kv, counts, w_out):
    dma = pltpu.SemaphoreType.DMA
    anywhere = pl.BlockSpec(memory_space=pl.ANY)
    both = dma((2, NG))
    one = dma((NG,))
    return pl.pallas_call(
        kernel,
        out_shape=jax.ShapeDtypeStruct((128, 1024), BF),
        in_specs=[anywhere, anywhere, anywhere, pl.BlockSpec(memory_space=pltpu.SMEM), anywhere],
        out_specs=pl.BlockSpec(memory_space=pltpu.VMEM),
        scratch_shapes=[
            pltpu.VMEM((NG, 2, 64, 1024), BF),
            pltpu.VMEM((1024, 512), BF),
            pltpu.VMEM((NK, NG, 2, 128, HD), BF),
            pltpu.VMEM((NG, NK, 2, 128, HD), BF),
            pltpu.VMEM((512, 1024), BF),
            pltpu.VMEM((2, NG, NK, 64, HD), BF),
            pltpu.VMEM((2, NG, 2, 64, HD), BF),
            pltpu.VMEM((2, NG, 2, 64, HD), BF),
            pltpu.VMEM((NG, NK, 64, HD), BF),
            pltpu.VMEM((NG, 64, HD), BF),
            pltpu.VMEM((2, NG, NK, 64, HD), BF),
            pltpu.VMEM((2, NG, 64, 1024), F32),
            pltpu.VMEM((2, NG, 64, 1024), BF),
            pltpu.VMEM((2, NG, 64, 1024), BF),
            pltpu.VMEM((2, 2, 8, 128), jnp.int32),
            pltpu.VMEM((NK, 2, 8, 128), jnp.int32),
            dma((8,)), dma((2, 2)), dma((NG, 2)), dma((NG, 2)),
            both, both, both, one, one, one, one,
            one, both, both, both, both, both, dma((2,)), dma((2,)), dma((2,)), dma((1,)),
        ],
        compiler_params=pltpu.CompilerParams(
            collective_id=0, has_side_effects=True, vmem_limit_bytes=60 * 1024 * 1024
        ),
        cost_estimate=pl.CostEstimate(flops=2_500_000_000, bytes_accessed=5_000_000, transcendentals=300_000),
    )(
        normed.reshape(2, 64, 1024),
        w_query.reshape(1024, 512),
        neighbour_kv.reshape(NG, 2, 128, 512),
        counts,
        w_out.reshape(512, 1024),
    )[None]


def solution(mesh):
    return jax.shard_map(
        on_device,
        mesh=mesh,
        in_specs=(
            P("pipe", "tensor", "dp"),
            P("pipe", "dp", "tensor"),
            P("dp", None, "pipe", None, None, "tensor"),
            P("pipe", "dp", None),
            P("pipe", "tensor", "dp"),
        ),
        out_specs=P("pipe", "tensor", "dp"),
        check_vma=False,
    )
```

```python
import math

import jax
import jax.numpy as jnp
from jax import lax
from jax.experimental import pallas as pl
from jax.experimental.pallas import tpu as pltpu
from jax.sharding import PartitionSpec as P

MESH = pl.DeviceIdType.MESH
BF = jnp.bfloat16
F32 = jnp.float32
HD = 128
NEG = -3.0e38
NG = 8
NK = 4
UNITS = 2 * NG
LAGS = (0, 2, 6, 10, 12)
BY_SPAN = False
STAG_AG = True
STAG_RS = True
AHEAD = 2
RING_AT = {}


def kernel(
    normed, wq_in, kv_in, counts, wo_in, out,
    xg, wq, kv, kvh, wo, qp, sib, qs, qin, att, ain, pm, rsb, rin, cnt_two, cnt,
    ld_sem, own_send, ag_send, ag_recv, sib_send, sib_recv, qs_send, qin_recv, kv_own, kv_send, kv_recv,
    at_send, at_recv, fw_send, fw_recv, rs_send, rs_recv, c2_send, c2_recv, cnt_send, cnt_recv,
):
    d = lax.axis_index("dp")
    p = lax.axis_index("pipe")
    t = lax.axis_index("tensor")
    zh = d // 2
    co = d % 2
    sibling = d + 1 - 2 * co
    c_own = p // NK
    k = p % NK
    up = (t + 1) % NG
    dn = (t + NG - 1) % NG
    on_diag = d == p
    query_self = on_diag & (k // 2 == co)

    def local(src, dst, sem):
        return pltpu.make_async_copy(src, dst, sem)

    def remote(src, dst, ssem, rsem, dev):
        return pltpu.make_async_remote_copy(
            src_ref=src, dst_ref=dst, send_sem=ssem, recv_sem=rsem, device_id=dev, device_id_type=MESH
        )

    def reach(src, dst, ssem, rsem, dev, is_self):
        @pl.when(is_self)
        def _():
            local(src, dst, rsem).start()

        @pl.when(jnp.logical_not(is_self))
        def _():
            remote(src, dst, ssem, rsem, dev).start()

    def await_bytes(ref, sem):
        local(ref, ref, sem).wait()

    loads = [
        local(normed.at[0], xg.at[0, 0], ld_sem.at[0]),
        local(normed.at[1], xg.at[0, 1], ld_sem.at[1]),
        local(wq_in, wq, ld_sem.at[2]),
        local(wo_in, wo, ld_sem.at[3]),
    ] + [local(kv_in.at[:, :, :, pl.ds(h * HD, HD)], kv.at[h], ld_sem.at[4 + h]) for h in range(NK)]
    for load in loads:
        load.start()

    barrier = pltpu.get_barrier_semaphore()

    def greet(dev):
        pl.semaphore_signal(barrier, inc=1, device_id=dev, device_id_type=MESH)

    def greet_other(dev, is_self):
        @pl.when(jnp.logical_not(is_self))
        def _():
            greet(dev)

    for n in range(NK):
        b = (n % 2) * NK + 2 * co + n // 2
        greet_other((p, b, t), on_diag & (b == p))
        source = 2 * n + k // 2
        greet_other((source, d, t), on_diag & (source == d))
    for n in range(1, NK):
        greet((d, c_own * NK + (k + n) % NK, t))
    greet((d, p, up))
    greet((d, p, dn))
    greet((sibling, p, t))
    for span in range(2):
        cnt_two[span, co] = jnp.full((8, 128), counts[0, 0, span], jnp.int32)
    pl.semaphore_wait(barrier, 14 - 2 * jnp.where(query_self, 1, 0))

    def send_own(half):
        loads[half].wait()
        remote(xg.at[0, half], xg.at[1, half], own_send.at[0, half], ag_recv.at[1, half], (d, p, up)).start()
        remote(xg.at[0, half], xg.at[2, half], own_send.at[1, half], ag_recv.at[2, half], (d, p, dn)).start()

    send_own(0)
    if not STAG_AG:
        send_own(1)
    for span in range(2):
        remote(
            cnt_two.at[span, co], cnt_two.at[span, co], c2_send.at[span], c2_recv.at[span], (sibling, p, t)
        ).start()
    for h in range(NK):
        loads[4 + h].wait()

    def sequence_of(i):
        hop = (i + 1) // 2
        return (t + NG + jnp.where(i % 2 == 1, -hop, hop)) % NG

    def along_x(n):
        return (d, c_own * NK + (k + n) % NK, t)

    def send_heads(i, carry):
        g = sequence_of(i)
        local(kv.at[k, g], kvh.at[i, k], kv_own.at[i]).start()
        for n in (1, 3, 2):
            remote(kv.at[(k + n) % NK, g], kvh.at[i, k], kv_send.at[i], kv_recv.at[i], along_x(n)).start()
        return carry

    lax.fori_loop(0, AHEAD, send_heads, 0)
    if STAG_AG:
        for way in range(2):
            await_bytes(xg.at[0, 0], own_send.at[way, 0])
        send_own(1)
    loads[2].wait()

    def project(c, i):
        @pl.when(i >= 1)
        def _():
            await_bytes(xg.at[i, c], ag_recv.at[i, c])
            upward = i % 2 == 1
            target = (d, p, jnp.where(upward, up, dn))
            later = jnp.minimum(i + 2, NG - 1)

            @pl.when((i <= 4) | (i == 5 + c))
            def _():
                remote(xg.at[i, c], xg.at[later, c], ag_send.at[i, c], ag_recv.at[later, c], target).start()

        @pl.when((c == 0) & (i < NG - AHEAD))
        def _():
            send_heads(i + AHEAD, 0)

        part = jnp.dot(xg[i, c], wq[...], preferred_element_type=F32).astype(BF)
        for h in range(NK):
            qp[c, i, h] = part[:, h * HD:(h + 1) * HD]
        remote(
            qp.at[c, i, pl.ds(2 - 2 * co, 2)], sib.at[c, i], sib_send.at[c, i], sib_recv.at[c, i], (sibling, p, t)
        ).start()

    def join_cores(c, i):
        @pl.when(i == 0)
        def _():
            await_bytes(cnt_two.at[c, co], c2_recv.at[c])
            for n in range(2):
                b = c * NK + 2 * co + n
                reach(cnt_two.at[c], cnt.at[zh], cnt_send.at[c], cnt_recv.at[0], (p, b, t), on_diag & (b == p))

        await_bytes(sib.at[c, i], sib_recv.at[c, i])
        for n in range(2):
            b = c * NK + 2 * co + n
            qs[c, i, n] = (qp[c, i, 2 * co + n].astype(F32) + sib[c, i, n].astype(F32)).astype(BF)
            reach(qs.at[c, i, n], qin.at[i, zh], qs_send.at[c, i], qin_recv.at[i], (p, b, t), on_diag & (b == p))

    def attend(c, i):
        @pl.when(i == 0)
        def _():
            await_bytes(cnt, cnt_recv.at[0])

        await_bytes(kvh.at[i, 0], kv_own.at[i])
        await_bytes(kvh.at[i, pl.ds(0, 3)], kv_recv.at[i])
        await_bytes(qin.at[i], qin_recv.at[i])
        total = qin[i, 0].astype(F32)
        for n in range(1, NK):
            total = total + qin[i, n].astype(F32)
        q = total.astype(BF)
        g = sequence_of(i)
        count = cnt[g // 2, g % 2][0:1, :]
        scores = []
        for n in range(NK):
            s = lax.dot_general(
                q, kvh[i, n, 0], (((1,), (1,)), ((), ())), preferred_element_type=F32
            ) * (1.0 / math.sqrt(HD))
            scores.append(jnp.where(count > n, s, NEG))
        top = jnp.max(
            jnp.maximum(jnp.maximum(scores[0], scores[1]), jnp.maximum(scores[2], scores[3])), axis=1, keepdims=True
        )
        e = [jnp.exp(s - top) for s in scores]
        den = jnp.sum((e[0] + e[1]) + (e[2] + e[3]), axis=1, keepdims=True)
        o = jnp.dot(e[0].astype(BF), kvh[i, 0, 1], preferred_element_type=F32)
        for n in range(1, NK):
            o = o + jnp.dot(e[n].astype(BF), kvh[i, n, 1], preferred_element_type=F32)
        att[i] = (o / den).astype(BF)
        for n in range(NK):
            dev = ((zh + n) % NK * 2 + k // 2, d, t)
            reach(
                att.at[i], ain.at[c_own, i, k], at_send.at[i], at_recv.at[c_own, i], dev,
                query_self & ((zh + n) % NK == zh),
            )

    def hand_over(c, i):
        pair = ain.at[c, i, pl.ds(2 * co, 2)]
        await_bytes(pair, at_recv.at[c, i])
        remote(pair, pair, fw_send.at[c, i], fw_recv.at[c, i], (sibling, p, t)).start()

    def mix(c, i):
        @pl.when((c == 0) & (i == 0))
        def _():
            loads[3].wait()

        await_bytes(ain.at[c, i, pl.ds(0, 2)], fw_recv.at[c, i])
        rows = jnp.concatenate([ain[c, i, h] for h in range(NK)], axis=1)
        pm[c, i] = jnp.dot(rows, wo[...], preferred_element_type=F32)

    def pass_on(c, slot, later, tensor_to, incoming):
        mine = pm[c, slot]
        if incoming:
            await_bytes(rin.at[c, slot], rs_recv.at[c, slot])
            mine = mine + rin[c, slot].astype(F32)
        rsb[c, slot] = mine.astype(BF)
        remote(
            rsb.at[c, slot], rin.at[c, later], rs_send.at[c, slot], rs_recv.at[c, later], (d, p, tensor_to)
        ).start()

    def ring(c, r):
        down = {1: (5, 3), 2: (3, 1), 3: (1, 0)}
        upward = {1: (6, 4), 2: (4, 2), 3: (2, 7)}
        if r == 0 and c == 0:
            pass_on(c, 7, 5, dn, False)
            pass_on(c, 6, 4, up, False)
            if STAG_RS:
                for slot in (7, 6):
                    await_bytes(rsb.at[c, slot], rs_send.at[c, slot])
        elif r == 0:
            pass_on(c, 7, 6, up, False)
            pass_on(c, 5, 3, dn, False)
        elif r == 1 and c == 0:
            pass_on(c, *down[r], dn, True)
        elif r == 1:
            pass_on(c, *upward[r], up, True)
        elif r < 4:
            pass_on(c, *down[r], dn, True)
            pass_on(c, *upward[r], up, True)
        else:
            await_bytes(rin.at[c, 0], rs_recv.at[c, 0])
            await_bytes(rin.at[c, 7], rs_recv.at[c, 7])
            out[c * 64:(c + 1) * 64] = (pm[c, 0] + rin[c, 0].astype(F32) + rin[c, 7].astype(F32)).astype(BF)

    stages = (
        (project, None), (join_cores, None), (attend, c_own), (hand_over, None), (mix, None),
    )

    def step(u, carry):
        for lag, (stage, only) in zip(LAGS, stages):
            v = u - lag
            c, i = (v // NG, v % NG) if BY_SPAN else (v % 2, v // 2)
            run = (v >= 0) & (v < UNITS)

            @pl.when(run if only is None else run & (c == only))
            def _():
                stage(c, i)

        for (c, r), at in RING_AT.items():
            @pl.when(u == at)
            def _():
                ring(c, r)

        return carry

    lax.fori_loop(0, UNITS + LAGS[-1], step, 0)
    for r in range(5):
        for c in range(2):
            if (c, r) not in RING_AT:
                ring(c, r)

    for way in range(2):
        for half in range(1 if STAG_AG else 0, 2):
            await_bytes(xg.at[0, half], own_send.at[way, half])
    for i in range(1, 7):
        for half in range(2):
            if i <= 4 or i == 5 + half:
                await_bytes(xg.at[i, half], ag_send.at[i, half])
    for c in range(2):
        await_bytes(cnt_two.at[c, co], c2_send.at[c])

    def drain(i, carry):
        for c in range(2):
            @pl.when((i >= 1) & (i < 6) if STAG_RS and c == 0 else (i >= 1))
            def _():
                await_bytes(rsb.at[c, i], rs_send.at[c, i])

            await_bytes(sib.at[c, i], sib_send.at[c, i])
            one_less = query_self & (c == c_own)

            @pl.when(one_less)
            def _():
                await_bytes(qs.at[c, i, 0], qs_send.at[c, i])

            @pl.when(jnp.logical_not(one_less))
            def _():
                await_bytes(qs.at[c, i], qs_send.at[c, i])

            @pl.when((i == 0) & one_less)
            def _():
                await_bytes(cnt.at[0], cnt_send.at[c])

            @pl.when((i == 0) & jnp.logical_not(one_less))
            def _():
                await_bytes(cnt.at[pl.ds(0, 2)], cnt_send.at[c])

        await_bytes(kvh.at[i, pl.ds(0, 3)], kv_send.at[i])

        @pl.when(query_self)
        def _():
            await_bytes(qin.at[i, pl.ds(0, 3)], at_send.at[i])

        @pl.when(jnp.logical_not(query_self))
        def _():
            await_bytes(qin.at[i], at_send.at[i])

        for c in range(2):
            await_bytes(ain.at[c, i, pl.ds(0, 2)], fw_send.at[c, i])
        return carry

    lax.fori_loop(0, NG, drain, 0)


def on_device(normed, w_query, neighbour_kv, counts, w_out):
    dma = pltpu.SemaphoreType.DMA
    anywhere = pl.BlockSpec(memory_space=pl.ANY)
    both = dma((2, NG))
    one = dma((NG,))
    return pl.pallas_call(
        kernel,
        out_shape=jax.ShapeDtypeStruct((128, 1024), BF),
        in_specs=[anywhere, anywhere, anywhere, pl.BlockSpec(memory_space=pltpu.SMEM), anywhere],
        out_specs=pl.BlockSpec(memory_space=pltpu.VMEM),
        scratch_shapes=[
            pltpu.VMEM((NG, 2, 64, 1024), BF),
            pltpu.VMEM((1024, 512), BF),
            pltpu.VMEM((NK, NG, 2, 128, HD), BF),
            pltpu.VMEM((NG, NK, 2, 128, HD), BF),
            pltpu.VMEM((512, 1024), BF),
            pltpu.VMEM((2, NG, NK, 64, HD), BF),
            pltpu.VMEM((2, NG, 2, 64, HD), BF),
            pltpu.VMEM((2, NG, 2, 64, HD), BF),
            pltpu.VMEM((NG, NK, 64, HD), BF),
            pltpu.VMEM((NG, 64, HD), BF),
            pltpu.VMEM((2, NG, NK, 64, HD), BF),
            pltpu.VMEM((2, NG, 64, 1024), F32),
            pltpu.VMEM((2, NG, 64, 1024), BF),
            pltpu.VMEM((2, NG, 64, 1024), BF),
            pltpu.VMEM((2, 2, 8, 128), jnp.int32),
            pltpu.VMEM((NK, 2, 8, 128), jnp.int32),
            dma((8,)), dma((2, 2)), dma((NG, 2)), dma((NG, 2)),
            both, both, both, one, one, one, one,
            one, both, both, both, both, both, dma((2,)), dma((2,)), dma((2,)), dma((1,)),
        ],
        compiler_params=pltpu.CompilerParams(
            collective_id=0, has_side_effects=True, vmem_limit_bytes=60 * 1024 * 1024
        ),
        cost_estimate=pl.CostEstimate(flops=2_500_000_000, bytes_accessed=5_000_000, transcendentals=300_000),
    )(
        normed.reshape(2, 64, 1024),
        w_query.reshape(1024, 512),
        neighbour_kv.reshape(NG, 2, 128, 512),
        counts,
        w_out.reshape(512, 1024),
    )[None]


def solution(mesh):
    return jax.shard_map(
        on_device,
        mesh=mesh,
        in_specs=(
            P("pipe", "tensor", "dp"),
            P("pipe", "dp", "tensor"),
            P("dp", None, "pipe", None, None, "tensor"),
            P("pipe", "dp", None),
            P("pipe", "tensor", "dp"),
        ),
        out_specs=P("pipe", "tensor", "dp"),
        check_vma=False,
    )
```
